256 devices in a mesh: row: 8 (over y, z_hi), col: 32 (over x, z_lo, core).
Axes of the slice: x: 4, y: 4, z: 8 (z_hi: 2, z_lo: 4; z = z_hi * 4 + z_lo), core: 2. Of those that a mesh axis runs over, the one named last changes fastest.
Arguments:
- a_values: bfloat16 [2, 12288, 4096], P(None, 'row', 'col'), may hold values from -0.44140625 to 0.44140625
- a_pattern: int32 [2, 96, 32], P(None, 'row', 'col'), may hold values 0 or 1
- c_mask: int32 [96, 96], P('row', 'col'), may hold values 0 or 1
Outputs:
- scores: float32 [12288, 12288], P('row', 'col')
The draws below stay inside these ranges and needn't reach their ends.
All inputs are finite; a program needn't handle non-finite values. No bound on the sum of `a_pattern` or of `c_mask` on one device may be relied on, other than what follows from the above.
Results may differ from the reference program's by a relative error of at most 0.0003.
Values may be sent and summed in bfloat16 or wider, within the bound.
A program may use at most 128 MiB of HBM per device.

```python
import jax
import jax.numpy as jnp
from jax import lax

TILE = 128
SECTIONS = 2
M = 12288
KP = 4096
MB = 96
N_COL = 32


def place_ends(array, key, low, top_value):
    extent = array.shape
    place = [jax.random.randint(jax.random.fold_in(key, axis), (), 0, extent[axis]) for axis in range(len(extent))]
    array = array.at[tuple(place)].set(low)
    longest = extent.index(max(extent))
    place[longest] = (place[longest] + 1) % extent[longest]
    return array.at[tuple(place)].set(top_value)


def steps_of(key, dims, cuts, low, high):
    loudness = 1.0
    for position, parts in cuts:
        draws = jax.random.uniform(jax.random.fold_in(jax.random.fold_in(key, 6), position), (parts,), jnp.float32, low / len(cuts), high / len(cuts))
        loudness = loudness * jnp.repeat(jnp.exp(draws), dims[position] // parts).reshape((-1,) + (1,) * (len(dims) - 1 - position))
    return loudness


def scatter_about(rng, dims, spread, limit, cuts=(), dtype=jnp.bfloat16):
    level = steps_of(rng, dims, cuts, -0.22, 0.18) if cuts else 1.0
    result = jax.random.normal(rng, dims, jnp.float32) * spread * level
    return jnp.minimum(jnp.maximum(result, -limit), limit).astype(dtype)


def setup_inputs(seed: int = 0) -> dict:
    streams_of = jax.random.split(jax.random.key(seed), 4)
    return {
        "a_values": scatter_about(streams_of[0], (SECTIONS, M, KP), (0.7 * (SECTIONS * KP) ** -0.25), 0.44140625, ((1, 8), (2, 32))),
        "a_pattern": place_ends((jax.random.randint(streams_of[1], (SECTIONS, MB, N_COL), 0, 2) < 1).astype(jnp.int32), jax.random.fold_in(streams_of[1], 1), 0, 1),
        "c_mask": place_ends((jax.random.randint(streams_of[2], (MB, MB), 0, 2) < 1).astype(jnp.int32), jax.random.fold_in(streams_of[2], 1), 0, 1),
    }


def spread_tiles(pattern):
    grown = jnp.repeat(pattern, TILE, axis=-2)
    return jnp.repeat(grown, TILE, axis=-1)


def reference(a_values, a_pattern, c_mask):
    live_tiles = a_values * spread_tiles(a_pattern).astype(jnp.bfloat16)
    full_sum = jnp.zeros((M, M), jnp.float32)
    for section in range(SECTIONS):
        panel = live_tiles[section].astype(jnp.float32)
        full_sum = full_sum + jnp.dot(panel, panel.T, precision=lax.Precision.HIGHEST)
    return full_sum * spread_tiles(c_mask).astype(jnp.float32)
```

```python
import functools

import jax
import jax.numpy as jnp
from jax import lax
from jax.experimental import pallas as pl
from jax.experimental.pallas import tpu as pltpu
from jax.sharding import PartitionSpec as P

TILE = 128
SECTIONS = 2
MESH = pl.DeviceIdType.MESH
LAST_TICK = 28


def kernel(rows, a_ref, pat_ref, mask_ref, out_ref, row, col, acc, got,
           zs, zr, xs, xr, ys, cr, cs, es, er):
    half, quarter = rows // 2, rows // 4
    width = half // 2
    tiles = rows // TILE

    row_id, col_id = lax.axis_index("row"), lax.axis_index("col")
    y, h = lax.div(row_id, 2), lax.rem(row_id, 2)
    x, zl, core = lax.div(col_id, 8), lax.rem(lax.div(col_id, 2), 4), lax.rem(col_id, 2)
    a, b = lax.div(zl, 2), lax.rem(zl, 2)
    x_up, x_down, x_far = lax.rem(x + 1, 4), lax.rem(x + 3, 4), lax.rem(x + 2, 4)
    ring = lax.rem(y - x + 4, 4)
    straight = h == a

    def device(x=x, y=y, h=h, zl=zl, core=core):
        return (y * 2 + h, x * 8 + zl * 2 + core)

    dev_x_up, dev_x_down = device(x=x_up), device(x=x_down)
    dev_y_up, dev_y_down = device(y=lax.rem(y + 1, 4)), device(y=lax.rem(y + 3, 4))
    dev_over, dev_core = device(h=1 - h), device(core=1 - core)
    z_peers = [lax.rem(zl + d, 4) for d in (1, 2, 3)]
    partners = [dev_x_up, dev_x_down, dev_y_up, dev_y_down, dev_over, dev_core]
    partners += [device(zl=z) for z in z_peers]

    barrier = pltpu.get_barrier_semaphore()
    for partner in partners:
        pl.semaphore_signal(barrier, inc=1, device_id=partner, device_id_type=MESH)

    own = x * 4 + zl

    def mask_tile(t, _):
        place = pl.ds(pl.multiple_of(t * TILE, TILE), TILE)
        for section in range(SECTIONS):
            keep = pat_ref[section, t, 0].astype(jnp.float32)
            tile = a_ref[section, place, :].astype(jnp.float32) * keep
            row[own, section, place, :] = tile.astype(jnp.bfloat16)
        return 0

    lax.fori_loop(0, tiles, mask_tile, 0)
    acc[...] = jnp.zeros_like(acc)
    pl.semaphore_wait(barrier, len(partners))

    def send(src, dst, send_sem, recv_sem, target):
        return pltpu.make_async_remote_copy(
            src_ref=src, dst_ref=dst, send_sem=send_sem, recv_sem=recv_sem,
            device_id=target, device_id_type=MESH)

    def row_half(s, g):
        return row.at[s, :, pl.ds(pl.multiple_of(g * half, half), half), :]

    def row_part(s, g, q):
        return row.at[s, :, pl.ds(pl.multiple_of(g * half + q * quarter, quarter), quarter), :]

    def col_part(s, q):
        return col.at[s, :, pl.ds(pl.multiple_of(q * quarter, quarter), quarter), :]

    def z_of(k):
        return 2 * lax.rem(a + lax.div(k, 2), 2) + lax.rem(b + lax.rem(k, 2), 2)

    def half_of(i):
        return lax.rem(b + lax.div(i, 4), 2)

    def wait_row(s, g, q):
        ref = row_part(s, g, q)
        send(ref, ref, xs.at[0, 0, 0], xr.at[s, g, q], dev_x_up).wait_recv()

    def wait_col(s, q):
        ref = col_part(s, q)
        send(ref, ref, xs.at[0, 0, 0], cr.at[s, q], dev_y_up).wait_recv()

    def send_item(i):
        s, g = x * 4 + z_of(lax.rem(i, 4)), half_of(i)
        for n, (way, q, target) in enumerate(
                ((0, 0, dev_x_up), (1, 1, dev_x_down), (0, 1, dev_x_up), (1, 0, dev_x_down))):
            ref = row_part(s, g, q)
            send(ref, ref, xs.at[way, i, n // 2], xr.at[s, g, q], target).start()

    send_item(jnp.int32(0))
    for late in range(2):
        for n, z in enumerate(z_peers):
            g = lax.rem(z + late, 2)
            ref = row_half(own, g)
            send(ref, ref, zs.at[late, n], zr.at[zl, g], device(zl=z)).start()

    def slice_of(n):
        o = lax.rem(n, 4)
        step = jnp.where(o == 0, 0, jnp.where(o == 1, 3, jnp.where(o == 2, 1, 2)))
        return lax.rem(x + step, 4) * 4 + z_of(lax.div(n, 4))

    def crossing(j, r, second):
        odd = lax.rem(r, 2)
        n = 4 * j + jnp.where(r == 0, 3, odd) + second * odd
        q = jnp.where(odd == 1, lax.div(r, 2), second)
        return slice_of(n), q

    def accumulate(group, f):
        g = lax.rem(b + f, 2)
        block = min(256, half)

        def one(t, _):
            place = pl.ds(pl.multiple_of(g * half + t * block, block), block)
            for side in range(2):
                total = acc[side, place, :]
                for o in range(4):
                    s = slice_of(group * 4 + o)
                    left = jnp.concatenate([row[s, 0, place, :], row[s, 1, place, :]], axis=1)
                    span = pl.ds(side * width, width)
                    right = jnp.concatenate([col[s, 0, span, :], col[s, 1, span, :]], axis=1)
                    total = total + lax.dot_general(
                        left, right, (((1,), (1,)), ((), ())), preferred_element_type=jnp.float32)
                acc[side, place, :] = total
            return 0

        lax.fori_loop(0, half // block, one, 0)

    def tick(m, _):
        i, sub = lax.div(m, 3), lax.rem(m, 3)

        @pl.when((sub == 0) & (i >= 1) & (i <= 8))
        def _():
            z, g = z_of(lax.rem(i - 1, 4)), half_of(i - 1)
            wait_row(x_down * 4 + z, g, 1)
            wait_row(x_up * 4 + z, g, 0)
            wait_row(x_far * 4 + z, g, 0)
            wait_row(x_far * 4 + z, g, 1)

        @pl.when((sub == 1) & (i < 8))
        def _():
            z, g = z_of(lax.rem(i, 4)), half_of(i)
            for way, q, source, target in ((0, 0, x_down, dev_x_up), (1, 1, x_up, dev_x_down)):
                s = source * 4 + z
                wait_row(s, g, q)
                ref = row_part(s, g, q)
                send(ref, ref, xs.at[way, i, 2], xr.at[s, g, q], target).start()

        @pl.when((sub == 2) & (i < 7))
        def _():
            @pl.when(lax.rem(i + 1, 4) != 0)
            def _():
                z, g = z_of(lax.rem(i + 1, 4)), half_of(i + 1)
                ref = row_half(x * 4 + z, g)
                send(ref, ref, xs.at[0, 0, 0], zr.at[z, g], dev_x_up).wait_recv()

            send_item(i + 1)

        @pl.when(straight)
        def _():
            @pl.when((ring == 0) & (m >= 2) & (m < 18))
            def _():
                s = slice_of(m - 2)
                col[s] = row[s, :, pl.ds(pl.multiple_of(b * half, half), half), :]
                for q, target in ((0, dev_y_up), (1, dev_y_down)):
                    send(row_part(s, b, q), col_part(s, q), ys.at[q, m - 2, 0], cr.at[s, q], target).start()

            for q, target in ((0, dev_y_up), (1, dev_y_down)):
                hops = ring if q == 0 else 4 - ring
                n = m - 2 - 2 * hops

                @pl.when((ring != 0) & (n >= 0) & (n < 16))
                def _():
                    s = slice_of(n)
                    wait_col(s, q)

                    @pl.when(hops < 3)
                    def _():
                        ref = col_part(s, q)
                        send(ref, ref, ys.at[q, n, 0], cr.at[s, q], target).start()

            @pl.when((m >= 6) & (m < 22) & (lax.rem(m, 4) == 2))
            def _():
                j = lax.div(m - 6, 4)
                for second in range(2):
                    s, q = crossing(j, ring, second)
                    ref = col_part(s, q)
                    send(ref, ref, cs.at[j, second], cr.at[s, q], dev_over).start()

            @pl.when((m >= 12) & (m < 28) & (lax.rem(m, 4) == 0))
            def _():
                accumulate(lax.div(m - 12, 4), 0)

            @pl.when((m >= 15) & (m < 27) & (sub == 0))
            def _():
                accumulate(lax.div(m - 15, 3), 1)

        @pl.when(jnp.logical_not(straight))
        def _():
            phase = lax.rem(m + 2, 4)
            r_down, r_up, r_far = lax.rem(ring + 3, 4), lax.rem(ring + 1, 4), lax.rem(ring + 2, 4)

            @pl.when((phase == 0) & (m >= 14))
            def _():
                j = lax.div(m - 14, 4)
                for r, second in ((r_down, 1), (r_up, 0), (r_far, 0), (r_far, 1)):
                    wait_col(*crossing(j, r, second))

            @pl.when((phase == 0) & (m >= 10) & (m < 26))
            def _():
                j = lax.div(m - 10, 4)
                parts = [crossing(j, ring, second) for second in range(2)]
                for s, q in parts:
                    wait_col(s, q)
                for n, (way, second, target) in enumerate(
                        ((0, 0, dev_y_up), (1, 1, dev_y_down), (0, 1, dev_y_up), (1, 0, dev_y_down))):
                    s, q = parts[second]
                    ref = col_part(s, q)
                    send(ref, ref, ys.at[way, j, n // 2], cr.at[s, q], target).start()

            @pl.when((phase == 2) & (m >= 12) & (m < 28))
            def _():
                j = lax.div(m - 12, 4)
                for way, r, target in ((0, r_down, dev_y_up), (1, r_up, dev_y_down)):
                    s, q = crossing(j, r, way)
                    wait_col(s, q)
                    ref = col_part(s, q)
                    send(ref, ref, ys.at[way, j, 2], cr.at[s, q], target).start()

            @pl.when((phase == 1) & (m >= 15))
            def _():
                accumulate(lax.div(m - 15, 4), 0)
                accumulate(lax.div(m - 15, 4), 1)

        return 0

    lax.fori_loop(0, LAST_TICK, tick, 0)

    def trade(f):
        g = lax.rem(b + f, 2)
        place = pl.ds(pl.multiple_of(g * half, half), half)
        return send(acc.at[1 - core, place, :], got.at[place, :], es.at[f], er.at[f], dev_core)

    trades = [trade(0), trade(1)]
    for one in trades:
        one.start()
    for f, one in enumerate(trades):
        one.wait_recv()
        first = lax.rem(b + f, 2) * (tiles // 2)

        def finish(t, _):
            tile_row = first + t
            place = pl.ds(pl.multiple_of(tile_row * TILE, TILE), TILE)
            for c in range(width // TILE):
                span = pl.ds(c * TILE, TILE)
                keep = mask_ref[tile_row, c].astype(jnp.float32)
                out_ref[place, span] = (acc[core, place, span] + got[place, span]) * keep
            return 0

        lax.fori_loop(0, tiles // 2, finish, 0)

    part = row_part(0, 0, 0)
    whole = row_half(0, 0)
    for one in trades:
        one.wait_send()
    for late in range(2):
        for n in range(3):
            send(whole, whole, zs.at[late, n], zr.at[0, 0], dev_x_up).wait_send()

    def drain_x(i, _):
        for way in range(2):
            for n in range(3):
                send(part, part, xs.at[way, i, n], xr.at[0, 0, 0], dev_x_up).wait_send()
        return 0

    lax.fori_loop(0, 8, drain_x, 0)

    @pl.when(straight)
    def _():
        def drain(n, _):
            for q in range(2):
                hops = ring if q == 0 else lax.rem(4 - ring, 4)

                @pl.when(hops < 3)
                def _():
                    send(part, part, ys.at[q, n, 0], xr.at[0, 0, 0], dev_x_up).wait_send()
            return 0

        lax.fori_loop(0, 16, drain, 0)

        def drain_over(j, _):
            for second in range(2):
                send(part, part, cs.at[j, second], xr.at[0, 0, 0], dev_x_up).wait_send()
            return 0

        lax.fori_loop(0, 4, drain_over, 0)

    @pl.when(jnp.logical_not(straight))
    def _():
        def drain(j, _):
            for way in range(2):
                for n in range(3):
                    send(part, part, ys.at[way, j, n], xr.at[0, 0, 0], dev_x_up).wait_send()
            return 0

        lax.fori_loop(0, 4, drain, 0)


def shards(a_values, a_pattern, c_mask):
    rows, depth = a_values.shape[1], a_values.shape[2]
    out_width = c_mask.shape[1] * TILE
    half = rows // 2
    vmem = pl.BlockSpec(memory_space=pltpu.VMEM)
    smem = pl.BlockSpec(memory_space=pltpu.SMEM)
    dma = pltpu.SemaphoreType.DMA
    return pl.pallas_call(
        functools.partial(kernel, rows),
        out_shape=jax.ShapeDtypeStruct((rows, out_width), jnp.float32),
        in_specs=[vmem, smem, smem],
        out_specs=vmem,
        scratch_shapes=[
            pltpu.VMEM((16, SECTIONS, rows, depth), jnp.bfloat16),
            pltpu.VMEM((16, SECTIONS, half, depth), jnp.bfloat16),
            pltpu.VMEM((2, rows, out_width), jnp.float32),
            pltpu.VMEM((rows, out_width), jnp.float32),
            dma((2, 3)), dma((4, 2)), dma((2, 8, 3)), dma((16, 2, 2)),
            dma((2, 16, 3)), dma((16, 2)), dma((4, 2)), dma((2,)), dma((2,)),
        ],
        compiler_params=pltpu.CompilerParams(
            collective_id=0, has_side_effects=True, vmem_limit_bytes=48 << 20),
        cost_estimate=pl.CostEstimate(
            flops=2 * rows * half * 16 * SECTIONS * depth, bytes_accessed=4 * rows * out_width, transcendentals=0),
        name="gather_and_multiply",
    )(a_values, a_pattern, c_mask)


def solution(mesh):
    return jax.shard_map(
        shards,
        mesh=mesh,
        in_specs=(P(None, "row", "col"), P(None, "row", "col"), P("row", "col")),
        out_specs=P("row", "col"),
        check_vma=False,
    )
```

```python
import functools

import jax
import jax.numpy as jnp
from jax import lax
from jax.experimental import pallas as pl
from jax.experimental.pallas import tpu as pltpu
from jax.sharding import PartitionSpec as P

TILE = 128
SECTIONS = 2
MESH = pl.DeviceIdType.MESH
LAST_TICK = 28


def kernel(rows, a_ref, pat_ref, mask_ref, out_ref, row, col, acc, got, relay, transit,
           zs, zr, xs, xr, ys, cr, cs, rr, tr, es, er):
    half, quarter = rows // 2, rows // 4
    width = half // 2
    tiles = rows // TILE

    row_id, col_id = lax.axis_index("row"), lax.axis_index("col")
    y, h = lax.div(row_id, 2), lax.rem(row_id, 2)
    x, zl, core = lax.div(col_id, 8), lax.rem(lax.div(col_id, 2), 4), lax.rem(col_id, 2)
    a, b = lax.div(zl, 2), lax.rem(zl, 2)
    x_up, x_down, x_far = lax.rem(x + 1, 4), lax.rem(x + 3, 4), lax.rem(x + 2, 4)
    ring = lax.rem(y - x + 4, 4)
    straight = h == a

    def device(x=x, y=y, h=h, zl=zl, core=core):
        return (y * 2 + h, x * 8 + zl * 2 + core)

    dev_x_up, dev_x_down = device(x=x_up), device(x=x_down)
    dev_y_up, dev_y_down = device(y=lax.rem(y + 1, 4)), device(y=lax.rem(y + 3, 4))
    dev_over, dev_core = device(h=1 - h, zl=2 * (1 - a) + b), device(core=1 - core)
    z_peers = [2 * lax.rem(a + k // 2, 2) + lax.rem(b + k % 2, 2) for k in (1, 2, 3)]
    partners = [dev_x_up, dev_x_down, dev_y_up, dev_y_down, dev_over, dev_core]
    partners += [device(zl=z) for z in z_peers]

    barrier = pltpu.get_barrier_semaphore()
    for partner in partners:
        pl.semaphore_signal(barrier, inc=1, device_id=partner, device_id_type=MESH)

    own = x * 4 + zl

    def mask_tile(t, _):
        place = pl.ds(pl.multiple_of(t * TILE, TILE), TILE)
        for section in range(SECTIONS):
            keep = pat_ref[section, t, 0].astype(jnp.float32)
            tile = a_ref[section, place, :].astype(jnp.float32) * keep
            row[own, section, place, :] = tile.astype(jnp.bfloat16)
        return 0

    lax.fori_loop(0, tiles, mask_tile, 0)
    acc[...] = jnp.zeros_like(acc)
    pl.semaphore_wait(barrier, len(partners))

    def send(src, dst, send_sem, recv_sem, target):
        return pltpu.make_async_remote_copy(
            src_ref=src, dst_ref=dst, send_sem=send_sem, recv_sem=recv_sem,
            device_id=target, device_id_type=MESH)

    def row_half(s, g):
        return row.at[s, :, pl.ds(pl.multiple_of(g * half, half), half), :]

    def row_part(s, g, q):
        return row.at[s, :, pl.ds(pl.multiple_of(g * half + q * quarter, quarter), quarter), :]

    def col_part(s, q):
        return col.at[s, :, pl.ds(pl.multiple_of(q * quarter, quarter), quarter), :]

    def z_of(k, first=a):
        return 2 * lax.rem(first + lax.div(k, 2), 2) + lax.rem(b + lax.rem(k, 2), 2)

    def half_of(i):
        return lax.rem(b + lax.div(i, 4), 2)

    def wait_row(s, g, q):
        ref = row_part(s, g, q)
        send(ref, ref, xs.at[0, 0, 0], xr.at[s, g, q], dev_x_up).wait_recv()

    def wait_col(s, q):
        ref = col_part(s, q)
        send(ref, ref, xs.at[0, 0, 0], cr.at[s, q], dev_y_up).wait_recv()

    def send_item(i):
        s, g = x * 4 + z_of(lax.rem(i, 4)), half_of(i)
        for n, (way, q, target) in enumerate(
                ((0, 0, dev_x_up), (1, 1, dev_x_down), (0, 1, dev_x_up), (1, 0, dev_x_down))):
            ref = row_part(s, g, q)
            send(ref, ref, xs.at[way, i, n // 2], xr.at[s, g, q], target).start()

    send_item(jnp.int32(0))
    def send_along_z(late, n):
        g = lax.rem(z_peers[n] + late, 2)
        ref = row_half(own, g)
        send(ref, ref, zs.at[late, n], zr.at[zl, g], device(zl=z_peers[n])).start()

    for n in range(3):
        send_along_z(0, n)

    def slice_of(n, first=h):
        o = lax.rem(n, 4)
        step = jnp.where(o == 0, 0, jnp.where(o == 1, 3, jnp.where(o == 2, 1, 2)))
        return lax.rem(x + step, 4) * 4 + z_of(lax.div(n, 4), first)

    def crossing(j, r, first=h):
        o = jnp.where(r == 0, 3, jnp.where(r == 2, 0, lax.div(r + 1, 2)))
        return slice_of(4 * j + o, first)

    def accumulate(group, f):
        g = lax.rem(b + f, 2)
        block = min(256, half)

        def one(t, _):
            place = pl.ds(pl.multiple_of(g * half + t * block, block), block)
            for side in range(2):
                total = acc[side, place, :]
                for o in range(4):
                    s = slice_of(group * 4 + o)
                    left = jnp.concatenate([row[s, 0, place, :], row[s, 1, place, :]], axis=1)
                    span = pl.ds(side * width, width)
                    right = jnp.concatenate([col[s, 0, span, :], col[s, 1, span, :]], axis=1)
                    total = total + lax.dot_general(
                        left, right, (((1,), (1,)), ((), ())), preferred_element_type=jnp.float32)
                acc[side, place, :] = total
            return 0

        lax.fori_loop(0, half // block, one, 0)

    def tick(m, _):
        i, sub = lax.div(m, 3), lax.rem(m, 3)

        @pl.when((sub == 0) & (i >= 1) & (i <= 8))
        def _():
            z, g = z_of(lax.rem(i - 1, 4)), half_of(i - 1)
            wait_row(x_down * 4 + z, g, 1)
            wait_row(x_up * 4 + z, g, 0)
            wait_row(x_far * 4 + z, g, 0)
            wait_row(x_far * 4 + z, g, 1)

        @pl.when((sub == 1) & (i < 8))
        def _():
            z, g = z_of(lax.rem(i, 4)), half_of(i)
            for way, q, source, target in ((0, 0, x_down, dev_x_up), (1, 1, x_up, dev_x_down)):
                s = source * 4 + z
                wait_row(s, g, q)
                ref = row_part(s, g, q)
                send(ref, ref, xs.at[way, i, 2], xr.at[s, g, q], target).start()

        @pl.when((sub == 2) & (i < 7))
        def _():
            @pl.when(lax.rem(i + 1, 4) != 0)
            def _():
                z, g = z_of(lax.rem(i + 1, 4)), half_of(i + 1)
                ref = row_half(x * 4 + z, g)
                send(ref, ref, xs.at[0, 0, 0], zr.at[z, g], dev_x_up).wait_recv()

            send_item(i + 1)

        for n in range(3):
            @pl.when(m == 7 + 3 * n)
            def _():
                send_along_z(1, n)

        @pl.when(straight)
        def _():
            @pl.when((ring == 0) & (m >= 2) & (m < 18))
            def _():
                s = slice_of(m - 2)
                col[s] = row[s, :, pl.ds(pl.multiple_of(b * half, half), half), :]
                for q, target in ((0, dev_y_up), (1, dev_y_down)):
                    send(row_part(s, b, q), col_part(s, q), ys.at[q, m - 2, 0], cr.at[s, q], target).start()

            for q, target in ((0, dev_y_up), (1, dev_y_down)):
                hops = ring if q == 0 else 4 - ring
                n = m - 2 - 2 * hops

                @pl.when((ring != 0) & (n >= 0) & (n < 16))
                def _():
                    s = slice_of(n)
                    wait_col(s, q)

                    @pl.when(hops < 3)
                    def _():
                        ref = col_part(s, q)
                        send(ref, ref, ys.at[q, n, 0], cr.at[s, q], target).start()

            @pl.when((m >= 12) & (m < 28) & (lax.rem(m, 4) == 0))
            def _():
                accumulate(lax.div(m - 12, 4), 0)

            @pl.when((m >= 15) & (m < 27) & (sub == 0))
            def _():
                accumulate(lax.div(m - 15, 3), 1)

        @pl.when(jnp.logical_not(straight))
        def _():
            phase = lax.rem(m + 2, 4)
            r_down, r_up, r_far = lax.rem(ring + 3, 4), lax.rem(ring + 1, 4), lax.rem(ring + 2, 4)

            @pl.when((ring == 0) & (m >= 2) & (m < 18))
            def _():
                j, o = lax.div(m - 2, 4), lax.rem(m - 2, 4)
                s = slice_of(m - 2, a)
                first, second = row_part(s, b, 0), row_part(s, b, 1)

                @pl.when(o == 0)
                def _():
                    send(first, transit.at[j], cs.at[j, 0], tr.at[j], dev_y_up).start()
                    send(second, transit.at[j], cs.at[j, 1], tr.at[j], dev_y_down).start()

                @pl.when(o == 1)
                def _():
                    send(first, relay.at[j, 0], cs.at[j, 2], rr.at[j, 0], dev_y_up).start()
                    send(second, relay.at[j, 1], cs.at[j, 3], rr.at[j, 1], dev_y_up).start()

                @pl.when(o == 2)
                def _():
                    send(first, relay.at[j, 0], cs.at[j, 4], rr.at[j, 0], dev_y_down).start()
                    send(second, relay.at[j, 1], cs.at[j, 5], rr.at[j, 1], dev_y_down).start()

                @pl.when(o == 3)
                def _():
                    send(first, col_part(s, 0), cs.at[j, 6], cr.at[s, 0], dev_over).start()
                    send(second, col_part(s, 1), cs.at[j, 7], cr.at[s, 1], dev_over).start()

            @pl.when((lax.rem(ring, 2) == 1) & (phase == 2) & (m >= 4) & (m < 20))
            def _():
                j = lax.div(m - 4, 4)
                send(transit.at[j], transit.at[j], cs.at[j, 0], tr.at[j], dev_y_up).wait_recv()

                @pl.when(ring == 1)
                def _():
                    send(transit.at[j], relay.at[j, 0], cs.at[j, 0], rr.at[j, 0], dev_y_up).start()

                @pl.when(ring == 3)
                def _():
                    send(transit.at[j], relay.at[j, 1], cs.at[j, 0], rr.at[j, 1], dev_y_down).start()

            @pl.when((ring != 0) & (phase == 1) & (m >= 7) & (m < 23))
            def _():
                j = lax.div(m - 7, 4)
                s = crossing(j, ring, a)
                for q in range(2):
                    ref = relay.at[j, q]
                    send(ref, ref, cs.at[j, 6 + q], rr.at[j, q], dev_over).wait_recv()
                    send(ref, col_part(s, q), cs.at[j, 6 + q], cr.at[s, q], dev_over).start()

            @pl.when((phase == 0) & (m >= 14))
            def _():
                j = lax.div(m - 14, 4)
                for r, q in ((r_down, 1), (r_up, 0), (r_far, 0), (r_far, 1)):
                    wait_col(crossing(j, r), q)

            @pl.when((phase == 0) & (m >= 10) & (m < 26))
            def _():
                j = lax.div(m - 10, 4)
                s = crossing(j, ring)
                for q in range(2):
                    wait_col(s, q)
                for n, (way, q, target) in enumerate(
                        ((0, 0, dev_y_up), (1, 1, dev_y_down), (0, 1, dev_y_up), (1, 0, dev_y_down))):
                    ref = col_part(s, q)
                    send(ref, ref, ys.at[way, j, n // 2], cr.at[s, q], target).start()

            @pl.when((phase == 2) & (m >= 12) & (m < 28))
            def _():
                j = lax.div(m - 12, 4)
                for way, r, target in ((0, r_down, dev_y_up), (1, r_up, dev_y_down)):
                    s = crossing(j, r)
                    wait_col(s, way)
                    ref = col_part(s, way)
                    send(ref, ref, ys.at[way, j, 2], cr.at[s, way], target).start()

            @pl.when((phase == 1) & (m >= 15))
            def _():
                accumulate(lax.div(m - 15, 4), 0)

            @pl.when(m >= 24)
            def _():
                accumulate(m - 24, 1)

        return 0

    lax.fori_loop(0, LAST_TICK, tick, 0)

    def trade(f):
        g = lax.rem(b + f, 2)
        place = pl.ds(pl.multiple_of(g * half, half), half)
        return send(acc.at[1 - core, place, :], got.at[place, :], es.at[f], er.at[f], dev_core)

    trades = [trade(0), trade(1)]
    for one in trades:
        one.start()
    for f, one in enumerate(trades):
        one.wait_recv()
        first = lax.rem(b + f, 2) * (tiles // 2)

        def finish(t, _):
            tile_row = first + t
            place = pl.ds(pl.multiple_of(tile_row * TILE, TILE), TILE)
            for c in range(width // TILE):
                span = pl.ds(c * TILE, TILE)
                keep = mask_ref[tile_row, c].astype(jnp.float32)
                out_ref[place, span] = (acc[core, place, span] + got[place, span]) * keep
            return 0

        lax.fori_loop(0, tiles // 2, finish, 0)

    part = row_part(0, 0, 0)
    whole = row_half(0, 0)
    for one in trades:
        one.wait_send()
    for late in range(2):
        for n in range(3):
            send(whole, whole, zs.at[late, n], zr.at[0, 0], dev_x_up).wait_send()

    def drain_x(i, _):
        for way in range(2):
            for n in range(3):
                send(part, part, xs.at[way, i, n], xr.at[0, 0, 0], dev_x_up).wait_send()
        return 0

    lax.fori_loop(0, 8, drain_x, 0)

    @pl.when(straight)
    def _():
        def drain(n, _):
            for q in range(2):
                hops = ring if q == 0 else lax.rem(4 - ring, 4)

                @pl.when(hops < 3)
                def _():
                    send(part, part, ys.at[q, n, 0], xr.at[0, 0, 0], dev_x_up).wait_send()
            return 0

        lax.fori_loop(0, 16, drain, 0)

    @pl.when(jnp.logical_not(straight))
    def _():
        def drain(j, _):
            for way in range(2):
                for n in range(3):
                    send(part, part, ys.at[way, j, n], xr.at[0, 0, 0], dev_x_up).wait_send()
            for n in range(8):
                @pl.when((ring == 0) | (n >= 6) | ((n == 0) & (ring != 2)))
                def _():
                    send(part, part, cs.at[j, n], xr.at[0, 0, 0], dev_x_up).wait_send()
            return 0

        lax.fori_loop(0, 4, drain, 0)


def shards(a_values, a_pattern, c_mask):
    rows, depth = a_values.shape[1], a_values.shape[2]
    out_width = c_mask.shape[1] * TILE
    half = rows // 2
    vmem = pl.BlockSpec(memory_space=pltpu.VMEM)
    smem = pl.BlockSpec(memory_space=pltpu.SMEM)
    dma = pltpu.SemaphoreType.DMA
    return pl.pallas_call(
        functools.partial(kernel, rows),
        out_shape=jax.ShapeDtypeStruct((rows, out_width), jnp.float32),
        in_specs=[vmem, smem, smem],
        out_specs=vmem,
        scratch_shapes=[
            pltpu.VMEM((16, SECTIONS, rows, depth), jnp.bfloat16),
            pltpu.VMEM((16, SECTIONS, half, depth), jnp.bfloat16),
            pltpu.VMEM((2, rows, out_width), jnp.float32),
            pltpu.VMEM((rows, out_width), jnp.float32),
            pltpu.VMEM((4, 2, SECTIONS, half // 2, depth), jnp.bfloat16),
            pltpu.VMEM((4, SECTIONS, half // 2, depth), jnp.bfloat16),
            dma((2, 3)), dma((4, 2)), dma((2, 8, 3)), dma((16, 2, 2)),
            dma((2, 16, 3)), dma((16, 2)), dma((4, 8)), dma((4, 2)), dma((4,)), dma((2,)), dma((2,)),
        ],
        compiler_params=pltpu.CompilerParams(
            collective_id=0, has_side_effects=True, vmem_limit_bytes=48 << 20),
        cost_estimate=pl.CostEstimate(
            flops=2 * rows * half * 16 * SECTIONS * depth, bytes_accessed=4 * rows * out_width, transcendentals=0),
        name="gather_and_multiply",
    )(a_values, a_pattern, c_mask)


def solution(mesh):
    return jax.shard_map(
        shards,
        mesh=mesh,
        in_specs=(P(None, "row", "col"), P(None, "row", "col"), P("row", "col")),
        out_specs=P("row", "col"),
        check_vma=False,
    )
```

```python
import functools

import jax
import jax.numpy as jnp
from jax import lax
from jax.experimental import pallas as pl
from jax.experimental.pallas import tpu as pltpu
from jax.sharding import PartitionSpec as P

TILE = 128
SECTIONS = 2
MESH = pl.DeviceIdType.MESH
START_Y = 2
EARLY_SCATTER, SCATTER, PASS_ON = (1, 3), (3, 3), (2, 4)
CROSS = (4, 4, 4)
GATHER = (8, 9, 8)
FORWARD, FORWARD_ROOT, FORWARD_OPPOSITE = 10, 11, 10
FINAL = 13
RELIEVED = 2
LATE_Z = (7, 10, 13)
LAST_TICK = 26


def kernel(rows, a_ref, pat_ref, mask_ref, out_ref, row, col, acc, got, relay, transit,
           zs, zr, xs, xr, ys, cr, cs, rr, tr, es, er, ls):
    half, quarter = rows // 2, rows // 4
    width = half // 2
    tiles = rows // TILE

    row_id, col_id = lax.axis_index("row"), lax.axis_index("col")
    y, h = lax.div(row_id, 2), lax.rem(row_id, 2)
    x, zl, core = lax.div(col_id, 8), lax.rem(lax.div(col_id, 2), 4), lax.rem(col_id, 2)
    a, b = lax.div(zl, 2), lax.rem(zl, 2)
    x_up, x_down, x_far = lax.rem(x + 1, 4), lax.rem(x + 3, 4), lax.rem(x + 2, 4)
    ring = lax.rem(y - x + 4, 4)
    straight = h == a

    def device(x=x, y=y, h=h, zl=zl, core=core):
        return (y * 2 + h, x * 8 + zl * 2 + core)

    dev_x_up, dev_x_down = device(x=x_up), device(x=x_down)
    dev_y_up, dev_y_down = device(y=lax.rem(y + 1, 4)), device(y=lax.rem(y + 3, 4))
    dev_over, dev_core = device(h=1 - h, zl=2 * (1 - a) + b), device(core=1 - core)
    z_peers = [2 * lax.rem(a + k // 2, 2) + lax.rem(b + k % 2, 2) for k in (1, 2, 3)]
    partners = [dev_x_up, dev_x_down, dev_y_up, dev_y_down, dev_over, dev_core]
    partners += [device(zl=z) for z in z_peers]

    barrier = pltpu.get_barrier_semaphore()
    for partner in partners:
        pl.semaphore_signal(barrier, inc=1, device_id=partner, device_id_type=MESH)

    own = x * 4 + zl

    load = pltpu.make_async_copy(a_ref, row.at[own], ls)
    load.start()
    load.wait()

    def mask_tile(t, _):
        place = pl.ds(pl.multiple_of(t * TILE, TILE), TILE)
        for section in range(SECTIONS):
            keep = pat_ref[section, 0, t].astype(jnp.float32)
            tile = row[own, section, place, :].astype(jnp.float32) * keep
            row[own, section, place, :] = tile.astype(jnp.bfloat16)
        return 0

    lax.fori_loop(0, tiles, mask_tile, 0)
    pl.semaphore_wait(barrier, len(partners))

    def send(src, dst, send_sem, recv_sem, target):
        return pltpu.make_async_remote_copy(
            src_ref=src, dst_ref=dst, send_sem=send_sem, recv_sem=recv_sem,
            device_id=target, device_id_type=MESH)

    def row_half(s, g):
        return row.at[s, :, pl.ds(pl.multiple_of(g * half, half), half), :]

    def row_part(s, g, q):
        return row.at[s, :, pl.ds(pl.multiple_of(g * half + q * quarter, quarter), quarter), :]

    def col_part(s, q):
        return col.at[s, :, pl.ds(pl.multiple_of(q * quarter, quarter), quarter), :]

    def z_of(k, first=a):
        return 2 * lax.rem(first + lax.div(k, 2), 2) + lax.rem(b + lax.rem(k, 2), 2)

    def item(i):
        k = lax.rem(i, 4)
        return k, z_of(k), lax.rem(b + lax.div(i, 4), 2)

    def wait_row(s, g, q):
        ref = row_part(s, g, q)
        send(ref, ref, xs.at[0, 0, 0], xr.at[s, g, q], dev_x_up).wait_recv()

    def wait_col(s, q):
        ref = col_part(s, q)
        send(ref, ref, xs.at[0, 0, 0], cr.at[s, q], dev_y_up).wait_recv()

    def send_item(i):
        _, z, g = item(i)
        s = x * 4 + z
        for n, (way, q, target) in enumerate(
                ((0, 0, dev_x_up), (1, 1, dev_x_down), (0, 1, dev_x_up), (1, 0, dev_x_down))):
            ref = row_part(s, g, q)
            send(ref, ref, xs.at[way, i, n // 2], xr.at[s, g, q], target).start()

    send_item(jnp.int32(0))
    def send_along_z(late, n):
        g = lax.rem(z_peers[n] + late, 2)
        ref = row_half(own, g)
        send(ref, ref, zs.at[late, n], zr.at[zl, g], device(zl=z_peers[n])).start()

    for n in range(3):
        send_along_z(0, n)
    acc[...] = jnp.zeros_like(acc)

    def slice_of(n, first=h):
        o = lax.rem(n, 4)
        step = jnp.where(o == 0, 0, jnp.where(o == 1, 3, jnp.where(o == 2, 1, 2)))
        return lax.rem(x + step, 4) * 4 + z_of(lax.div(n, 4), first)

    def crossing(j, r, first=h):
        o = jnp.where(r == 0, 3, jnp.where(r == 2, 0, lax.div(r + 1, 2)))
        return slice_of(4 * j + o, first)

    def accumulate(group, f):
        place = pl.ds(pl.multiple_of(lax.rem(b + f, 2) * half, half), half)
        slices = [slice_of(group * 4 + o) for o in range(4)]
        left = jnp.concatenate([row[s, e, place, :] for s in slices for e in range(SECTIONS)], axis=1)
        right = jnp.concatenate([col[s, e] for s in slices for e in range(SECTIONS)], axis=1)
        total = lax.dot_general(left, right, (((1,), (1,)), ((), ())), preferred_element_type=jnp.float32)
        for side in range(2):
            acc[side, place, :] += total[:, side * width:(side + 1) * width]

    def tick(m, _):
        i, sub = lax.div(m, 3), lax.rem(m, 3)

        @pl.when((sub == 0) & (i >= 1) & (i <= 8))
        def _():
            _, z, g = item(i - 1)
            wait_row(x_down * 4 + z, g, 1)
            wait_row(x_up * 4 + z, g, 0)
            wait_row(x_far * 4 + z, g, 0)
            wait_row(x_far * 4 + z, g, 1)

        @pl.when((sub == 1) & (i < 8))
        def _():
            _, z, g = item(i)
            for way, q, source, target in ((0, 0, x_down, dev_x_up), (1, 1, x_up, dev_x_down)):
                s = source * 4 + z
                wait_row(s, g, q)
                ref = row_part(s, g, q)
                send(ref, ref, xs.at[way, i, 2], xr.at[s, g, q], target).start()

        @pl.when((sub == 2) & (i < 7))
        def _():
            k, z, g = item(i + 1)

            @pl.when(k != 0)
            def _():
                ref = row_half(x * 4 + z, g)
                send(ref, ref, xs.at[0, 0, 0], zr.at[z, g], dev_x_up).wait_recv()

            send_item(i + 1)

        for n in range(3):
            @pl.when(m == LATE_Z[n])
            def _():
                send_along_z(1, n)

        @pl.when(straight)
        def _():
            @pl.when((ring == 0) & (m >= START_Y) & (m < START_Y + 16))
            def _():
                s = slice_of(m - START_Y)
                col[s] = row[s, :, pl.ds(pl.multiple_of(b * half, half), half), :]
                for q, target in ((0, dev_y_up), (1, dev_y_down)):
                    send(row_part(s, b, q), col_part(s, q), ys.at[q, m - START_Y, 0], cr.at[s, q], target).start()

            for q, target in ((0, dev_y_up), (1, dev_y_down)):
                hops = ring if q == 0 else 4 - ring
                n = m - START_Y - 2 * hops

                @pl.when((ring != 0) & (n >= 0) & (n < 16))
                def _():
                    s = slice_of(n)
                    wait_col(s, q)

                    @pl.when(hops < 3)
                    def _():
                        ref = col_part(s, q)
                        send(ref, ref, ys.at[q, n, 0], cr.at[s, q], target).start()

        @pl.when(jnp.logical_not(straight))
        def _():
            def at(when):
                first, step = when if isinstance(when, tuple) else (when, 4)
                since = m - first + 4 * step
                here = (m >= first) & (m < first + 4 * step) & (lax.rem(since, step) == 0)
                return here, lax.div(since, step) - 4

            def by_place(ticks):
                return jnp.where(ring == 0, ticks[0], jnp.where(ring == 2, ticks[2], ticks[1]))

            r_down, r_up, r_far = lax.rem(ring + 3, 4), lax.rem(ring + 1, 4), lax.rem(ring + 2, 4)
            beside = lax.rem(ring, 2) == 1

            def scatter(j, jobs):
                for n, r, q, dst, recv_sem, target in jobs:
                    send(row_part(crossing(j, r, a), b, q), dst, cs.at[j, n], recv_sem, target).start()

            here, j = at(EARLY_SCATTER)

            @pl.when((ring == 0) & here)
            def _():
                scatter(j, ((0, 2, 0, transit.at[j], tr.at[j], dev_y_up),
                            (1, 2, 1, transit.at[j], tr.at[j], dev_y_down)))

            here, j = at(SCATTER)

            @pl.when((ring == 0) & here)
            def _():
                jobs = []
                for q in range(2):
                    jobs.append((2 + q, 1, q, relay.at[j, q], rr.at[j, q], dev_y_up))
                    jobs.append((4 + q, 3, q, relay.at[j, q], rr.at[j, q], dev_y_down))
                s = crossing(j, 0, a)
                for q in range(2):
                    jobs.append((6 + q, 0, q, col_part(s, q), cr.at[s, q], dev_over))
                scatter(j, jobs)

            here, j = at(PASS_ON)

            @pl.when(beside & here)
            def _():
                send(transit.at[j], transit.at[j], cs.at[j, 0], tr.at[j], dev_y_up).wait_recv()

                @pl.when(ring == 1)
                def _():
                    send(transit.at[j], relay.at[j, 0], cs.at[j, 0], rr.at[j, 0], dev_y_up).start()

                @pl.when(ring == 3)
                def _():
                    send(transit.at[j], relay.at[j, 1], cs.at[j, 0], rr.at[j, 1], dev_y_down).start()

            here, j = at(by_place(CROSS))

            @pl.when((ring != 0) & here)
            def _():
                s = crossing(j, ring, a)
                for q in range(2):
                    ref = relay.at[j, q]
                    send(ref, ref, cs.at[j, 6 + q], rr.at[j, q], dev_over).wait_recv()
                    send(ref, col_part(s, q), cs.at[j, 6 + q], cr.at[s, q], dev_over).start()

            here, j = at(by_place(GATHER))

            @pl.when(here)
            def _():
                s = crossing(j, ring)
                for q in range(2):
                    wait_col(s, q)
                for n, (way, q, target) in enumerate(
                        ((0, 0, dev_y_up), (1, 1, dev_y_down), (0, 1, dev_y_up), (1, 0, dev_y_down))):
                    ref = col_part(s, q)
                    send(ref, ref, ys.at[way, j, n // 2], cr.at[s, q], target).start()

            for way, r, target in ((0, r_down, dev_y_up), (1, r_up, dev_y_down)):
                here, j = at(jnp.where(beside, jnp.where(r == 0, FORWARD_ROOT, FORWARD_OPPOSITE), FORWARD))

                @pl.when(here)
                def _():
                    s = crossing(j, r)
                    wait_col(s, way)

                    @pl.when((ring != 0) | (j >= RELIEVED))
                    def _():
                        ref = col_part(s, way)
                        send(ref, ref, ys.at[way, j, 2], cr.at[s, way], target).start()

                    @pl.when((ring == 2) & (j < RELIEVED))
                    def _():
                        wait_col(s, 1 - way)
                        ref = col_part(s, 1 - way)
                        send(ref, ref, ys.at[way, j, 3], cr.at[s, 1 - way], target).start()

            here, j = at(FINAL)

            @pl.when(here)
            def _():
                @pl.when((ring != 2) | (j >= RELIEVED))
                def _():
                    for way, r in ((0, r_down), (1, r_up)):
                        wait_col(crossing(j, r), 1 - way)

                for q in range(2):
                    wait_col(crossing(j, r_far), q)

        start = jnp.where(straight, 12, FINAL + 1)
        first_due = (m >= start) & (m < start + 12) & (lax.rem(m + 16 - start, 4) == 0)
        second_due = jnp.where(straight, (m >= 15) & (m < 24) & (sub == 0), (m == 21) | (m == 23) | (m == 24))
        second = jnp.where(straight, i - 5, jnp.where(m == 21, 0, jnp.where(m == 23, 2, 1)))

        def product(f, _):
            @pl.when(jnp.where(f == 0, first_due, second_due))
            def _():
                accumulate(jnp.where(f == 0, lax.div(m + 16 - start, 4) - 4, second), f)
            return 0

        lax.fori_loop(0, 2, product, 0)
        return 0

    lax.fori_loop(0, LAST_TICK, tick, 0)

    def trade(f):
        g = lax.rem(b + f, 2)
        place = pl.ds(pl.multiple_of(g * half, half), half)
        return send(acc.at[1 - core, place, :], got.at[place, :], es.at[f], er.at[f], dev_core)

    def last(f, _):
        accumulate(3, f)
        trade(f).start()
        return 0

    lax.fori_loop(0, 2, last, 0)

    def settle(f, _):
        trade(f).wait_recv()
        first = lax.rem(b + f, 2) * (tiles // 2)

        def finish(t, _):
            tile_row = first + t
            place = pl.ds(pl.multiple_of(tile_row * TILE, TILE), TILE)
            for c in range(width // TILE):
                span = pl.ds(c * TILE, TILE)
                keep = mask_ref[c, tile_row].astype(jnp.float32)
                out_ref[place, span] = (acc[core, place, span] + got[place, span]) * keep
            return 0

        lax.fori_loop(0, tiles // 2, finish, 0)
        trade(f).wait_send()
        return 0

    lax.fori_loop(0, 2, settle, 0)

    part = row_part(0, 0, 0)
    whole = row_half(0, 0)
    for late in range(2):
        for n in range(3):
            send(whole, whole, zs.at[late, n], zr.at[0, 0], dev_x_up).wait_send()

    def drain_x(i, _):
        for way in range(2):
            for n in range(3):
                send(part, part, xs.at[way, i, n], xr.at[0, 0, 0], dev_x_up).wait_send()
        return 0

    lax.fori_loop(0, 8, drain_x, 0)

    @pl.when(straight)
    def _():
        def drain(n, _):
            for q in range(2):
                hops = ring if q == 0 else lax.rem(4 - ring, 4)

                @pl.when(hops < 3)
                def _():
                    send(part, part, ys.at[q, n, 0], xr.at[0, 0, 0], dev_x_up).wait_send()
            return 0

        lax.fori_loop(0, 16, drain, 0)

    @pl.when(jnp.logical_not(straight))
    def _():
        def drain(j, _):
            for way in range(2):
                for n in range(4):
                    done = (n < 2) | ((n == 2) & ((ring != 0) | (j >= RELIEVED)))

                    @pl.when(done | ((n == 3) & (ring == 2) & (j < RELIEVED)))
                    def _():
                        send(part, part, ys.at[way, j, n], xr.at[0, 0, 0], dev_x_up).wait_send()
            for n in range(8):
                @pl.when((ring == 0) | (n >= 6) | ((n == 0) & (ring != 2)))
                def _():
                    send(part, part, cs.at[j, n], xr.at[0, 0, 0], dev_x_up).wait_send()
            return 0

        lax.fori_loop(0, 4, drain, 0)


def shards(a_values, a_pattern, c_mask):
    rows, depth = a_values.shape[1], a_values.shape[2]
    out_width = c_mask.shape[1] * TILE
    half = rows // 2
    vmem = pl.BlockSpec(memory_space=pltpu.VMEM)
    smem = pl.BlockSpec(memory_space=pltpu.SMEM)
    dma = pltpu.SemaphoreType.DMA
    return pl.pallas_call(
        functools.partial(kernel, rows),
        out_shape=jax.ShapeDtypeStruct((rows, out_width), jnp.float32),
        in_specs=[pl.BlockSpec(memory_space=pl.ANY), smem, smem],
        out_specs=vmem,
        scratch_shapes=[
            pltpu.VMEM((16, SECTIONS, rows, depth), jnp.bfloat16),
            pltpu.VMEM((16, SECTIONS, half, depth), jnp.bfloat16),
            pltpu.VMEM((2, rows, out_width), jnp.float32),
            pltpu.VMEM((rows, out_width), jnp.float32),
            pltpu.VMEM((4, 2, SECTIONS, half // 2, depth), jnp.bfloat16),
            pltpu.VMEM((4, SECTIONS, half // 2, depth), jnp.bfloat16),
            dma((2, 3)), dma((4, 2)), dma((2, 8, 3)), dma((16, 2, 2)),
            dma((2, 16, 4)), dma((16, 2)), dma((4, 8)), dma((4, 2)), dma((4,)), dma((2,)), dma((2,)), dma,
        ],
        compiler_params=pltpu.CompilerParams(
            collective_id=0, has_side_effects=True, vmem_limit_bytes=48 << 20),
        cost_estimate=pl.CostEstimate(
            flops=2 * rows * half * 16 * SECTIONS * depth, bytes_accessed=4 * rows * out_width, transcendentals=0),
        name="gather_and_multiply",
    )(a_values, a_pattern.transpose(0, 2, 1), c_mask.T)


def solution(mesh):
    return jax.shard_map(
        shards,
        mesh=mesh,
        in_specs=(P(None, "row", "col"), P(None, "row", "col"), P("row", "col")),
        out_specs=P("row", "col"),
        check_vma=False,
    )
```

```python
import functools

import jax
import jax.numpy as jnp
from jax import lax
from jax.experimental import pallas as pl
from jax.experimental.pallas import tpu as pltpu
from jax.sharding import PartitionSpec as P

TILE = 128
SECTIONS = 2
MESH = pl.DeviceIdType.MESH
START_Y = 2
EARLY_SCATTER, SCATTER, PASS_ON = (1, 3), (3, 3), (2, 4)
CROSS = (4, 4, 4)
GATHER = (8, 9, 8)
FORWARD, FORWARD_ROOT, FORWARD_OPPOSITE = 10, 11, 10
FINAL = 13
RELIEVED = 2
LATE_Z = (7, 10, 13)
LAST_TICK = 24


def kernel(rows, a_ref, pat_hbm, mask_hbm, out_ref, pat_ref, mask_ref, row, col, acc, got, relay, transit,
           zs, zr, xs, xr, ys, cr, cs, rr, tr, es, er, ls):
    half, quarter = rows // 2, rows // 4
    width = half // 2
    tiles = rows // TILE

    row_id, col_id = lax.axis_index("row"), lax.axis_index("col")
    y, h = lax.div(row_id, 2), lax.rem(row_id, 2)
    x, zl, core = lax.div(col_id, 8), lax.rem(lax.div(col_id, 2), 4), lax.rem(col_id, 2)
    a, b = lax.div(zl, 2), lax.rem(zl, 2)
    x_up, x_down, x_far = lax.rem(x + 1, 4), lax.rem(x + 3, 4), lax.rem(x + 2, 4)
    ring = lax.rem(y - x + 4, 4)
    straight = h == a

    def device(x=x, y=y, h=h, zl=zl, core=core):
        return (y * 2 + h, x * 8 + zl * 2 + core)

    dev_x_up, dev_x_down = device(x=x_up), device(x=x_down)
    dev_y_up, dev_y_down = device(y=lax.rem(y + 1, 4)), device(y=lax.rem(y + 3, 4))
    dev_over, dev_core = device(h=1 - h, zl=2 * (1 - a) + b), device(core=1 - core)
    z_peers = [2 * lax.rem(a + k // 2, 2) + lax.rem(b + k % 2, 2) for k in (1, 2, 3)]
    partners = [dev_x_up, dev_x_down, dev_y_up, dev_y_down, dev_over, dev_core]
    partners += [device(zl=z) for z in z_peers]

    barrier = pltpu.get_barrier_semaphore()
    for partner in partners:
        pl.semaphore_signal(barrier, inc=1, device_id=partner, device_id_type=MESH)

    own = x * 4 + zl

    loads = [pltpu.make_async_copy(src, dst, ls.at[n]) for n, (src, dst) in enumerate(
        ((a_ref, row.at[own]), (pat_hbm, pat_ref), (mask_hbm, mask_ref)))]
    for load in loads:
        load.start()
    for load in loads:
        load.wait()

    def mask_tile(t, _):
        place = pl.ds(pl.multiple_of(t * TILE, TILE), TILE)
        for section in range(SECTIONS):
            keep = pat_ref[section, 0, t].astype(jnp.float32)
            tile = row[own, section, place, :].astype(jnp.float32) * keep
            row[own, section, place, :] = tile.astype(jnp.bfloat16)
        return 0

    lax.fori_loop(0, tiles, mask_tile, 0)
    pl.semaphore_wait(barrier, len(partners))

    def send(src, dst, send_sem, recv_sem, target):
        return pltpu.make_async_remote_copy(
            src_ref=src, dst_ref=dst, send_sem=send_sem, recv_sem=recv_sem,
            device_id=target, device_id_type=MESH)

    def row_half(s, g):
        return row.at[s, :, pl.ds(pl.multiple_of(g * half, half), half), :]

    def row_part(s, g, q):
        return row.at[s, :, pl.ds(pl.multiple_of(g * half + q * quarter, quarter), quarter), :]

    def col_part(s, q):
        return col.at[s, :, pl.ds(pl.multiple_of(q * quarter, quarter), quarter), :]

    def z_of(k, first=a):
        return 2 * lax.rem(first + lax.div(k, 2), 2) + lax.rem(b + lax.rem(k, 2), 2)

    def item(i):
        k = lax.rem(i, 4)
        return k, z_of(k), lax.rem(b + lax.div(i, 4), 2)

    def wait_row(s, g, q):
        ref = row_part(s, g, q)
        send(ref, ref, xs.at[0, 0, 0], xr.at[s, g, q], dev_x_up).wait_recv()

    def wait_col(s, q):
        ref = col_part(s, q)
        send(ref, ref, xs.at[0, 0, 0], cr.at[s, q], dev_y_up).wait_recv()

    def send_item(i):
        _, z, g = item(i)
        s = x * 4 + z
        for n, (way, q, target) in enumerate(
                ((0, 0, dev_x_up), (1, 1, dev_x_down), (0, 1, dev_x_up), (1, 0, dev_x_down))):
            ref = row_part(s, g, q)
            send(ref, ref, xs.at[way, i, n // 2], xr.at[s, g, q], target).start()

    send_item(jnp.int32(0))
    for n in range(3):
        g = lax.rem(z_peers[n], 2)
        ref = row_half(own, g)
        send(ref, ref, zs.at[0, n], zr.at[zl, g], device(zl=z_peers[n])).start()

    def pass_along_z(k, way):
        to = zl + 1 - 2 * way
        block = 2 * lax.rem(lax.div(to + 4, 2) + k // 2, 2) + lax.rem(to + 4 + k % 2, 2)
        due = (to >= 0) & (to < 4) & ((block <= zl) if way == 0 else (block >= zl))
        ref = row_half(x * 4 + block, b)
        return due, send(ref, ref, zs.at[1 + way, k - 1], zr.at[block, b], device(zl=lax.rem(to + 4, 4)))
    acc[...] = jnp.zeros_like(acc)

    def slice_of(n, first=h):
        o = lax.rem(n, 4)
        step = jnp.where(o == 0, 0, jnp.where(o == 1, 3, jnp.where(o == 2, 1, 2)))
        return lax.rem(x + step, 4) * 4 + z_of(lax.div(n, 4), first)

    def crossing(j, r, first=h):
        o = jnp.where(r == 0, 3, jnp.where(r == 2, 0, lax.div(r + 1, 2)))
        return slice_of(4 * j + o, first)

    def accumulate(slices, f):
        place = pl.ds(pl.multiple_of(lax.rem(b + f, 2) * half, half), half)
        left = jnp.concatenate([row[s, e, place, :] for s in slices for e in range(SECTIONS)], axis=1)
        right = jnp.concatenate([col[s, e] for s in slices for e in range(SECTIONS)], axis=1)
        total = lax.dot_general(left, right, (((1,), (1,)), ((), ())), preferred_element_type=jnp.float32)
        for side in range(2):
            acc[side, place, :] += total[:, side * width:(side + 1) * width]

    def group_slices(group):
        return [slice_of(group * 4 + o) for o in range(4)]

    r_down, r_up, r_far = lax.rem(ring + 3, 4), lax.rem(ring + 1, 4), lax.rem(ring + 2, 4)

    def wait_near_rows(i):
        _, z, g = item(i)
        wait_row(x_down * 4 + z, g, 1)
        wait_row(x_up * 4 + z, g, 0)

    def wait_far_rows(i):
        _, z, g = item(i)
        wait_row(x_far * 4 + z, g, 0)
        wait_row(x_far * 4 + z, g, 1)

    def wait_near_columns(j):
        for way, r in ((0, r_down), (1, r_up)):
            wait_col(crossing(j, r), 1 - way)

    def wait_far_columns(j):
        for q in range(2):
            wait_col(crossing(j, r_far), q)

    def tick(m, _):
        i, sub = lax.div(m, 3), lax.rem(m, 3)

        @pl.when((sub == 0) & (i >= 1))
        def _():
            wait_near_rows(i - 1)
            wait_far_rows(i - 1)

        @pl.when((sub == 1) & (i < 8))
        def _():
            _, z, g = item(i)
            for way, q, source, target in ((0, 0, x_down, dev_x_up), (1, 1, x_up, dev_x_down)):
                s = source * 4 + z
                wait_row(s, g, q)
                ref = row_part(s, g, q)
                send(ref, ref, xs.at[way, i, 2], xr.at[s, g, q], target).start()

        @pl.when((sub == 2) & (i < 7))
        def _():
            k, z, g = item(i + 1)

            @pl.when(k != 0)
            def _():
                ref = row_half(x * 4 + z, g)
                send(ref, ref, xs.at[0, 0, 0], zr.at[z, g], dev_x_up).wait_recv()

            send_item(i + 1)

        for k in (1, 2, 3):
            for way in range(2):
                due, one = pass_along_z(k, way)

                @pl.when(due & (m == LATE_Z[k - 1]))
                def _():
                    one.start()

        @pl.when(straight)
        def _():
            @pl.when((ring == 0) & (m >= START_Y) & (m < START_Y + 16))
            def _():
                s = slice_of(m - START_Y)
                col[s] = row[s, :, pl.ds(pl.multiple_of(b * half, half), half), :]
                for q, target in ((0, dev_y_up), (1, dev_y_down)):
                    send(row_part(s, b, q), col_part(s, q), ys.at[q, m - START_Y, 0], cr.at[s, q], target).start()

            for q, target in ((0, dev_y_up), (1, dev_y_down)):
                hops = ring if q == 0 else 4 - ring
                n = m - START_Y - 2 * hops

                @pl.when((ring != 0) & (n >= 0) & (n < 16))
                def _():
                    s = slice_of(n)
                    wait_col(s, q)

                    @pl.when(hops < 3)
                    def _():
                        ref = col_part(s, q)
                        send(ref, ref, ys.at[q, n, 0], cr.at[s, q], target).start()

        @pl.when(jnp.logical_not(straight))
        def _():
            def at(when):
                first, step = when if isinstance(when, tuple) else (when, 4)
                since = m - first + 4 * step
                here = (m >= first) & (m < first + 4 * step) & (lax.rem(since, step) == 0)
                return here, lax.div(since, step) - 4

            def by_place(ticks):
                return jnp.where(ring == 0, ticks[0], jnp.where(ring == 2, ticks[2], ticks[1]))

            beside = lax.rem(ring, 2) == 1

            def scatter(j, jobs):
                for n, r, q, dst, recv_sem, target in jobs:
                    send(row_part(crossing(j, r, a), b, q), dst, cs.at[j, n], recv_sem, target).start()

            here, j = at(EARLY_SCATTER)

            @pl.when((ring == 0) & here)
            def _():
                scatter(j, ((0, 2, 0, transit.at[j], tr.at[j], dev_y_up),
                            (1, 2, 1, transit.at[j], tr.at[j], dev_y_down)))

            here, j = at(SCATTER)

            @pl.when((ring == 0) & here)
            def _():
                jobs = []
                for q in range(2):
                    jobs.append((2 + q, 1, q, relay.at[j, q], rr.at[j, q], dev_y_up))
                    jobs.append((4 + q, 3, q, relay.at[j, q], rr.at[j, q], dev_y_down))
                s = crossing(j, 0, a)
                for q in range(2):
                    jobs.append((6 + q, 0, q, col_part(s, q), cr.at[s, q], dev_over))
                scatter(j, jobs)

            here, j = at(PASS_ON)

            @pl.when(beside & here)
            def _():
                send(transit.at[j], transit.at[j], cs.at[j, 0], tr.at[j], dev_y_up).wait_recv()

                @pl.when(ring == 1)
                def _():
                    send(transit.at[j], relay.at[j, 0], cs.at[j, 0], rr.at[j, 0], dev_y_up).start()

                @pl.when(ring == 3)
                def _():
                    send(transit.at[j], relay.at[j, 1], cs.at[j, 0], rr.at[j, 1], dev_y_down).start()

            here, j = at(by_place(CROSS))

            @pl.when((ring != 0) & here)
            def _():
                s = crossing(j, ring, a)
                for q in range(2):
                    ref = relay.at[j, q]
                    send(ref, ref, cs.at[j, 6 + q], rr.at[j, q], dev_over).wait_recv()
                    send(ref, col_part(s, q), cs.at[j, 6 + q], cr.at[s, q], dev_over).start()

            here, j = at(by_place(GATHER))

            @pl.when(here)
            def _():
                s = crossing(j, ring)
                for q in range(2):
                    wait_col(s, q)
                for n, (way, q, target) in enumerate(
                        ((0, 0, dev_y_up), (1, 1, dev_y_down), (0, 1, dev_y_up), (1, 0, dev_y_down))):
                    ref = col_part(s, q)
                    send(ref, ref, ys.at[way, j, n // 2], cr.at[s, q], target).start()

            for way, r, target in ((0, r_down, dev_y_up), (1, r_up, dev_y_down)):
                here, j = at(jnp.where(beside, jnp.where(r == 0, FORWARD_ROOT, FORWARD_OPPOSITE), FORWARD))

                @pl.when(here)
                def _():
                    s = crossing(j, r)
                    wait_col(s, way)

                    @pl.when((ring != 0) | (j >= RELIEVED))
                    def _():
                        ref = col_part(s, way)
                        send(ref, ref, ys.at[way, j, 2], cr.at[s, way], target).start()

                    @pl.when((ring == 2) & (j < RELIEVED))
                    def _():
                        wait_col(s, 1 - way)
                        ref = col_part(s, 1 - way)
                        send(ref, ref, ys.at[way, j, 3], cr.at[s, 1 - way], target).start()

            here, j = at(FINAL)

            @pl.when(here)
            def _():
                @pl.when((ring != 2) | (j >= RELIEVED))
                def _():
                    wait_near_columns(j)

                wait_far_columns(j)

        start = jnp.where(straight, 12, FINAL + 1)
        first_due = (m >= start) & (m < start + 12) & (lax.rem(m + 16 - start, 4) == 0)
        second_due = jnp.where(straight, (m >= 15) & (m < 24) & (sub == 0), (m == 21) | (m == 23))
        second = jnp.where(straight, i - 5, jnp.where(m == 21, 0, 2))

        def product(f, _):
            @pl.when(jnp.where(f == 0, first_due, second_due))
            def _():
                accumulate(group_slices(jnp.where(f == 0, lax.div(m + 16 - start, 4) - 4, second)), f)
            return 0

        lax.fori_loop(0, 2, product, 0)
        return 0

    lax.fori_loop(0, LAST_TICK, tick, 0)

    def trade(f):
        g = lax.rem(b + f, 2)
        place = pl.ds(pl.multiple_of(g * half, half), half)
        return send(acc.at[1 - core, place, :], got.at[place, :], es.at[f], er.at[f], dev_core)

    @pl.when(jnp.logical_not(straight))
    def _():
        wait_near_rows(7)
        wait_far_rows(7)

    accumulate([jnp.where(straight, p, q) for p, q in zip(group_slices(3), group_slices(1))], jnp.where(straight, 0, 1))

    @pl.when(straight)
    def _():
        trade(0).start()
        wait_near_rows(7)

    @pl.when(jnp.logical_not(straight))
    def _():
        wait_near_columns(3)

    ends = [jnp.where(straight, slice_of(12 + o), crossing(3, lax.rem(ring + turn, 4)))
            for o, turn in ((0, 0), (1, 3), (2, 1), (3, 2))]
    first_half = jnp.where(straight, 1, 0)

    def nearly(f, _):
        accumulate(ends[:3], f)
        return 0

    lax.fori_loop(first_half, 2, nearly, 0)

    @pl.when(straight)
    def _():
        wait_far_rows(7)

    @pl.when(jnp.logical_not(straight))
    def _():
        wait_far_columns(3)

    def last(f, _):
        accumulate(ends[3:], f)
        trade(f).start()
        return 0

    lax.fori_loop(first_half, 2, last, 0)

    def settle(f, _):
        trade(f).wait_recv()
        first = lax.rem(b + f, 2) * (tiles // 2)

        def finish(t, _):
            tile_row = first + t
            place = pl.ds(pl.multiple_of(tile_row * TILE, TILE), TILE)
            for c in range(width // TILE):
                span = pl.ds(c * TILE, TILE)
                keep = mask_ref[c, tile_row].astype(jnp.float32)
                out_ref[place, span] = (acc[core, place, span] + got[place, span]) * keep
            return 0

        lax.fori_loop(0, tiles // 2, finish, 0)
        trade(f).wait_send()
        return 0

    lax.fori_loop(0, 2, settle, 0)

    part = row_part(0, 0, 0)
    whole = row_half(0, 0)
    for n in range(3):
        send(whole, whole, zs.at[0, n], zr.at[0, 0], dev_x_up).wait_send()
        for way in range(2):
            due, one = pass_along_z(n + 1, way)

            @pl.when(due)
            def _():
                one.wait_send()

    def drain_x(i, _):
        for way in range(2):
            for n in range(3):
                send(part, part, xs.at[way, i, n], xr.at[0, 0, 0], dev_x_up).wait_send()
        return 0

    lax.fori_loop(0, 8, drain_x, 0)

    @pl.when(straight)
    def _():
        def drain(n, _):
            for q in range(2):
                hops = ring if q == 0 else lax.rem(4 - ring, 4)

                @pl.when(hops < 3)
                def _():
                    send(part, part, ys.at[q, n, 0], xr.at[0, 0, 0], dev_x_up).wait_send()
            return 0

        lax.fori_loop(0, 16, drain, 0)

    @pl.when(jnp.logical_not(straight))
    def _():
        def drain(j, _):
            for way in range(2):
                for n in range(4):
                    done = (n < 2) | ((n == 2) & ((ring != 0) | (j >= RELIEVED)))

                    @pl.when(done | ((n == 3) & (ring == 2) & (j < RELIEVED)))
                    def _():
                        send(part, part, ys.at[way, j, n], xr.at[0, 0, 0], dev_x_up).wait_send()
            for n in range(8):
                @pl.when((ring == 0) | (n >= 6) | ((n == 0) & (ring != 2)))
                def _():
                    send(part, part, cs.at[j, n], xr.at[0, 0, 0], dev_x_up).wait_send()
            return 0

        lax.fori_loop(0, 4, drain, 0)


def shards(a_values, a_pattern, c_mask):
    rows, depth = a_values.shape[1], a_values.shape[2]
    out_width = c_mask.shape[1] * TILE
    half = rows // 2
    vmem = pl.BlockSpec(memory_space=pltpu.VMEM)
    dma = pltpu.SemaphoreType.DMA
    return pl.pallas_call(
        functools.partial(kernel, rows),
        out_shape=jax.ShapeDtypeStruct((rows, out_width), jnp.float32),
        in_specs=[pl.BlockSpec(memory_space=pl.ANY)] * 3,
        out_specs=vmem,
        scratch_shapes=[
            pltpu.SMEM((SECTIONS, 1, rows // TILE), jnp.int32),
            pltpu.SMEM((c_mask.shape[1], rows // TILE), jnp.int32),
            pltpu.VMEM((16, SECTIONS, rows, depth), jnp.bfloat16),
            pltpu.VMEM((16, SECTIONS, half, depth), jnp.bfloat16),
            pltpu.VMEM((2, rows, out_width), jnp.float32),
            pltpu.VMEM((rows, out_width), jnp.float32),
            pltpu.VMEM((4, 2, SECTIONS, half // 2, depth), jnp.bfloat16),
            pltpu.VMEM((4, SECTIONS, half // 2, depth), jnp.bfloat16),
            dma((3, 3)), dma((4, 2)), dma((2, 8, 3)), dma((16, 2, 2)),
            dma((2, 16, 4)), dma((16, 2)), dma((4, 8)), dma((4, 2)), dma((4,)), dma((2,)), dma((2,)), dma((3,)),
        ],
        compiler_params=pltpu.CompilerParams(
            collective_id=0, has_side_effects=True, vmem_limit_bytes=48 << 20),
        cost_estimate=pl.CostEstimate(
            flops=2 * rows * half * 16 * SECTIONS * depth, bytes_accessed=4 * rows * out_width, transcendentals=0),
        name="gather_and_multiply",
    )(a_values, a_pattern.transpose(0, 2, 1), c_mask.T)


def solution(mesh):
    return jax.shard_map(
        shards,
        mesh=mesh,
        in_specs=(P(None, "row", "col"), P(None, "row", "col"), P("row", "col")),
        out_specs=P("row", "col"),
        check_vma=False,
    )
```

```python
import functools

import jax
import jax.numpy as jnp
from jax import lax
from jax.experimental import pallas as pl
from jax.experimental.pallas import tpu as pltpu
from jax.sharding import PartitionSpec as P

TILE = 128
SECTIONS = 2
MESH = pl.DeviceIdType.MESH
START_Y = 2
EARLY_SCATTER, SCATTER, PASS_ON = (1, 3), (3, 3), (2, 4)
CROSS = (4, 4, 4)
GATHER = (8, 9, 8)
FORWARD, FORWARD_ROOT, FORWARD_OPPOSITE = 10, 11, 10
FINAL = 13
RELIEVED = 2
EARLY_Z = (0, 1)
LATE_Z = (8, 11, 14)
LAST_TICK = 24


def kernel(rows, a_ref, pat_hbm, mask_hbm, out_ref, pat_ref, mask_ref, row, col, acc, got, relay, transit, other_row, other_col,
           zs, zr, xs, xr, ys, cr, cs, rr, tr, es, er, ls):
    half, quarter = rows // 2, rows // 4
    width = half // 2
    tiles = rows // TILE

    row_id, col_id = lax.axis_index("row"), lax.axis_index("col")
    y, h = lax.div(row_id, 2), lax.rem(row_id, 2)
    x, zl, core = lax.div(col_id, 8), lax.rem(lax.div(col_id, 2), 4), lax.rem(col_id, 2)
    a, b = lax.div(zl, 2), lax.rem(zl, 2)
    x_up, x_down, x_far = lax.rem(x + 1, 4), lax.rem(x + 3, 4), lax.rem(x + 2, 4)
    ring = lax.rem(y - x + 4, 4)
    straight = h == a

    def device(x=x, y=y, h=h, zl=zl, core=core):
        return (y * 2 + h, x * 8 + zl * 2 + core)

    dev_x_up, dev_x_down = device(x=x_up), device(x=x_down)
    dev_y_up, dev_y_down = device(y=lax.rem(y + 1, 4)), device(y=lax.rem(y + 3, 4))
    dev_over, dev_core = device(h=1 - h, zl=2 * (1 - a) + b), device(core=1 - core)
    z_peers = [2 * lax.rem(a + k // 2, 2) + lax.rem(b + k % 2, 2) for k in (1, 2, 3)]
    partners = [dev_x_up, dev_x_down, dev_y_up, dev_y_down, dev_over, dev_core]
    partners += [device(zl=z) for z in z_peers]

    barrier = pltpu.get_barrier_semaphore()
    for partner in partners:
        pl.semaphore_signal(barrier, inc=1, device_id=partner, device_id_type=MESH)

    own = x * 4 + zl

    loads = [pltpu.make_async_copy(src, dst, ls.at[n]) for n, (src, dst) in enumerate(
        ((a_ref, row.at[own]), (pat_hbm, pat_ref), (mask_hbm, mask_ref)))]
    for load in loads:
        load.start()
    for load in loads:
        load.wait()

    def mask_tile(t, _):
        place = pl.ds(pl.multiple_of(t * TILE, TILE), TILE)
        for section in range(SECTIONS):
            keep = pat_ref[section, 0, t].astype(jnp.float32)
            tile = row[own, section, place, :].astype(jnp.float32) * keep
            row[own, section, place, :] = tile.astype(jnp.bfloat16)
        return 0

    lax.fori_loop(0, tiles, mask_tile, 0)
    pl.semaphore_wait(barrier, len(partners))

    def send(src, dst, send_sem, recv_sem, target):
        return pltpu.make_async_remote_copy(
            src_ref=src, dst_ref=dst, send_sem=send_sem, recv_sem=recv_sem,
            device_id=target, device_id_type=MESH)

    def row_half(s, g):
        return row.at[s, :, pl.ds(pl.multiple_of(g * half, half), half), :]

    def row_part(s, g, q):
        return row.at[s, :, pl.ds(pl.multiple_of(g * half + q * quarter, quarter), quarter), :]

    def col_part(s, q):
        return col.at[s, :, pl.ds(pl.multiple_of(q * quarter, quarter), quarter), :]

    def z_of(k, first=a):
        return 2 * lax.rem(first + lax.div(k, 2), 2) + lax.rem(b + lax.rem(k, 2), 2)

    def item(i):
        k = lax.rem(i, 4)
        return k, z_of(k), lax.rem(b + lax.div(i, 4), 2)

    def wait_row(s, g, q):
        ref = row_part(s, g, q)
        send(ref, ref, xs.at[0, 0, 0], xr.at[s, g, q], dev_x_up).wait_recv()

    def wait_col(s, q):
        ref = col_part(s, q)
        send(ref, ref, xs.at[0, 0, 0], cr.at[s, q], dev_y_up).wait_recv()

    def send_item(i):
        _, z, g = item(i)
        s = x * 4 + z
        for n, (way, q, target) in enumerate(
                ((0, 0, dev_x_up), (1, 1, dev_x_down), (0, 1, dev_x_up), (1, 0, dev_x_down))):
            ref = row_part(s, g, q)
            send(ref, ref, xs.at[way, i, n // 2], xr.at[s, g, q], target).start()

    send_item(jnp.int32(0))
    def send_along_z(n):
        g = lax.rem(z_peers[n], 2)
        ref = row_half(own, g)
        send(ref, ref, zs.at[0, n], zr.at[zl, g], device(zl=z_peers[n])).start()

    send_along_z(0)

    def pass_along_z(k, way):
        to = zl + 1 - 2 * way
        block = 2 * lax.rem(lax.div(to + 4, 2) + k // 2, 2) + lax.rem(to + 4 + k % 2, 2)
        due = (to >= 0) & (to < 4) & ((block <= zl) if way == 0 else (block >= zl))
        ref = row_half(x * 4 + block, b)
        return due, send(ref, ref, zs.at[1 + way, k - 1], zr.at[block, b], device(zl=lax.rem(to + 4, 4)))
    acc[...] = jnp.zeros_like(acc)

    def slice_of(n, first=h):
        o = lax.rem(n, 4)
        step = jnp.where(o == 0, 0, jnp.where(o == 1, 3, jnp.where(o == 2, 1, 2)))
        return lax.rem(x + step, 4) * 4 + z_of(lax.div(n, 4), first)

    def crossing(j, r, first=h):
        o = jnp.where(r == 0, 3, jnp.where(r == 2, 0, lax.div(r + 1, 2)))
        return slice_of(4 * j + o, first)

    def accumulate(slices, f):
        place = pl.ds(pl.multiple_of(lax.rem(b + f, 2) * half, half), half)
        left = jnp.concatenate([row[s, e, place, :] for s in slices for e in range(SECTIONS)], axis=1)
        right = jnp.concatenate([col[s, e] for s in slices for e in range(SECTIONS)], axis=1)
        total = lax.dot_general(left, right, (((1,), (1,)), ((), ())), preferred_element_type=jnp.float32)
        for side in range(2):
            acc[side, place, :] += total[:, side * width:(side + 1) * width]

    def group_slices(group):
        return [slice_of(group * 4 + o) for o in range(4)]

    r_down, r_up, r_far = lax.rem(ring + 3, 4), lax.rem(ring + 1, 4), lax.rem(ring + 2, 4)

    def wait_near_rows(i):
        _, z, g = item(i)
        wait_row(x_down * 4 + z, g, 1)
        wait_row(x_up * 4 + z, g, 0)

    def wait_far_rows(i):
        _, z, g = item(i)
        wait_row(x_far * 4 + z, g, 0)
        wait_row(x_far * 4 + z, g, 1)

    def wait_near_columns(j):
        for way, r in ((0, r_down), (1, r_up)):
            wait_col(crossing(j, r), 1 - way)

    def wait_far_columns(j):
        for q in range(2):
            wait_col(crossing(j, r_far), q)

    def scatter(j, jobs):
        for n, r, q, dst, recv_sem, target in jobs:
            send(row_part(crossing(j, r, a), b, q), dst, cs.at[j, n], recv_sem, target).start()

    def scatter_near(j):
        jobs = []
        for q in range(2):
            jobs.append((2 + q, 1, q, relay.at[j, q], rr.at[j, q], dev_y_up))
            jobs.append((4 + q, 3, q, relay.at[j, q], rr.at[j, q], dev_y_down))
        scatter(j, jobs)

    scatters = jnp.logical_not(straight) & (ring == 0)

    def tick(m, _):
        i, sub = lax.div(m, 3), lax.rem(m, 3)

        @pl.when((sub == 0) & (i >= 1))
        def _():
            wait_near_rows(i - 1)

            @pl.when(scatters & (i <= 4))
            def _():
                scatter_near(i - 1)

            wait_far_rows(i - 1)

        @pl.when((sub == 1) & (i < 8))
        def _():
            _, z, g = item(i)
            for way, q, source, target in ((0, 0, x_down, dev_x_up), (1, 1, x_up, dev_x_down)):
                s = source * 4 + z
                wait_row(s, g, q)
                ref = row_part(s, g, q)
                send(ref, ref, xs.at[way, i, 2], xr.at[s, g, q], target).start()

        @pl.when((sub == 2) & (i < 7))
        def _():
            k, z, g = item(i + 1)

            @pl.when(k != 0)
            def _():
                ref = row_half(x * 4 + z, g)
                send(ref, ref, xs.at[0, 0, 0], zr.at[z, g], dev_x_up).wait_recv()

            send_item(i + 1)

        for n in (1, 2):
            @pl.when(m == EARLY_Z[n - 1])
            def _():
                send_along_z(n)

        for k in (1, 2, 3):
            for way in range(2):
                due, one = pass_along_z(k, way)

                @pl.when(due & (m == LATE_Z[k - 1]))
                def _():
                    one.start()

        @pl.when(straight)
        def _():
            @pl.when((ring == 0) & (m >= START_Y) & (m < START_Y + 16))
            def _():
                s = slice_of(m - START_Y)
                col[s] = row[s, :, pl.ds(pl.multiple_of(b * half, half), half), :]
                for q, target in ((0, dev_y_up), (1, dev_y_down)):
                    send(row_part(s, b, q), col_part(s, q), ys.at[q, m - START_Y, 0], cr.at[s, q], target).start()

            for q, target in ((0, dev_y_up), (1, dev_y_down)):
                hops = ring if q == 0 else 4 - ring
                n = m - START_Y - 2 * hops

                @pl.when((ring != 0) & (n >= 0) & (n < 16))
                def _():
                    s = slice_of(n)
                    wait_col(s, q)

                    @pl.when(hops < 3)
                    def _():
                        ref = col_part(s, q)
                        send(ref, ref, ys.at[q, n, 0], cr.at[s, q], target).start()

        @pl.when(jnp.logical_not(straight))
        def _():
            def at(when):
                first, step = when if isinstance(when, tuple) else (when, 4)
                since = m - first + 4 * step
                here = (m >= first) & (m < first + 4 * step) & (lax.rem(since, step) == 0)
                return here, lax.div(since, step) - 4

            def by_place(ticks):
                return jnp.where(ring == 0, ticks[0], jnp.where(ring == 2, ticks[2], ticks[1]))

            beside = lax.rem(ring, 2) == 1

            here, j = at(EARLY_SCATTER)

            @pl.when((ring == 0) & here)
            def _():
                scatter(j, ((0, 2, 0, transit.at[j], tr.at[j], dev_y_up),
                            (1, 2, 1, transit.at[j], tr.at[j], dev_y_down)))

            here, j = at(SCATTER)

            @pl.when((ring == 0) & here)
            def _():
                jobs = []
                s = crossing(j, 0, a)
                for q in range(2):
                    jobs.append((6 + q, 0, q, col_part(s, q), cr.at[s, q], dev_over))
                scatter(j, jobs)

            here, j = at(PASS_ON)

            @pl.when(beside & here)
            def _():
                send(transit.at[j], transit.at[j], cs.at[j, 0], tr.at[j], dev_y_up).wait_recv()

                @pl.when(ring == 1)
                def _():
                    send(transit.at[j], relay.at[j, 0], cs.at[j, 0], rr.at[j, 0], dev_y_up).start()

                @pl.when(ring == 3)
                def _():
                    send(transit.at[j], relay.at[j, 1], cs.at[j, 0], rr.at[j, 1], dev_y_down).start()

            here, j = at(by_place(CROSS))

            @pl.when((ring != 0) & here)
            def _():
                s = crossing(j, ring, a)
                for q in range(2):
                    ref = relay.at[j, q]
                    send(ref, ref, cs.at[j, 6 + q], rr.at[j, q], dev_over).wait_recv()
                    send(ref, col_part(s, q), cs.at[j, 6 + q], cr.at[s, q], dev_over).start()

            here, j = at(by_place(GATHER))

            @pl.when(here)
            def _():
                s = crossing(j, ring)
                for q in range(2):
                    wait_col(s, q)
                for n, (way, q, target) in enumerate(
                        ((0, 0, dev_y_up), (1, 1, dev_y_down), (0, 1, dev_y_up), (1, 0, dev_y_down))):
                    ref = col_part(s, q)
                    send(ref, ref, ys.at[way, j, n // 2], cr.at[s, q], target).start()

            for way, r, target in ((0, r_down, dev_y_up), (1, r_up, dev_y_down)):
                here, j = at(jnp.where(beside, jnp.where(r == 0, FORWARD_ROOT, FORWARD_OPPOSITE), FORWARD))

                @pl.when(here)
                def _():
                    s = crossing(j, r)
                    wait_col(s, way)

                    @pl.when((ring != 0) | (j >= RELIEVED))
                    def _():
                        ref = col_part(s, way)
                        send(ref, ref, ys.at[way, j, 2], cr.at[s, way], target).start()

                    @pl.when((ring == 2) & (j < RELIEVED))
                    def _():
                        wait_col(s, 1 - way)
                        ref = col_part(s, 1 - way)
                        send(ref, ref, ys.at[way, j, 3], cr.at[s, 1 - way], target).start()

            here, j = at(FINAL)

            @pl.when(here)
            def _():
                @pl.when((ring != 2) | (j >= RELIEVED))
                def _():
                    wait_near_columns(j)

                wait_far_columns(j)

        start = jnp.where(straight, 12, FINAL + 1)
        first_due = (m >= start) & (m < start + 12) & (lax.rem(m + 16 - start, 4) == 0)
        second_due = jnp.where(straight, (m >= 15) & (m < 24) & (sub == 0), (m == 21) | (m == 23))
        second = jnp.where(straight, i - 5, jnp.where(m == 21, 0, 2))

        def product(f, _):
            @pl.when(jnp.where(f == 0, first_due, second_due))
            def _():
                accumulate(group_slices(jnp.where(f == 0, lax.div(m + 16 - start, 4) - 4, second)), f)
            return 0

        lax.fori_loop(0, 2, product, 0)
        return 0

    lax.fori_loop(0, LAST_TICK, tick, 0)

    def trade(f):
        g = lax.rem(b + f, 2)
        place = pl.ds(pl.multiple_of(g * half, half), half)
        return send(acc.at[1 - core, place, :], got.at[place, :], es.at[f], er.at[f], dev_core)

    @pl.when(jnp.logical_not(straight))
    def _():
        wait_near_rows(7)
        wait_far_rows(7)

    ends = [jnp.where(straight, slice_of(12 + o), crossing(3, lax.rem(ring + turn, 4)))
            for o, turn in ((0, 0), (1, 3), (2, 1), (3, 2))]
    final = ends[3]

    def half_place(f):
        return pl.ds(pl.multiple_of(lax.rem(b + f, 2) * half, half), half)

    def give_rows(f, n):
        place = half_place(f)
        return send(row.at[final, :, place, :], other_row.at[:, place, :], es.at[n], er.at[n], dev_core)

    def give_columns(n):
        return send(col.at[final], other_col, es.at[n], er.at[n], dev_core)

    @pl.when(straight)
    def _():
        give_columns(2).start()

    @pl.when(jnp.logical_not(straight))
    def _():
        give_rows(0, 2).start()
        give_rows(1, 3).start()

    accumulate([jnp.where(straight, p, q) for p, q in zip(group_slices(3), group_slices(1))], jnp.where(straight, 0, 1))

    @pl.when(straight)
    def _():
        trade(0).start()
        wait_near_rows(7)

    @pl.when(jnp.logical_not(straight))
    def _():
        wait_near_columns(3)

    first_half = jnp.where(straight, 1, 0)

    def nearly(f, _):
        accumulate(ends[:3], f)
        trade(f).start()
        return 0

    lax.fori_loop(first_half, 2, nearly, 0)

    @pl.when(straight)
    def _():
        wait_far_rows(7)
        give_rows(1, 4).start()
        give_columns(2).wait_recv()
        give_rows(1, 4).wait_recv()

    @pl.when(jnp.logical_not(straight))
    def _():
        wait_far_columns(3)
        give_columns(4).start()
        give_rows(0, 2).wait_recv()
        give_rows(1, 3).wait_recv()
        give_columns(4).wait_recv()

    def last(f, _):
        place = half_place(f)
        span = pl.ds(pl.multiple_of(core * width, width), width)
        left = jnp.concatenate([row[final, e, place, :] for e in range(SECTIONS)]
                               + [other_row[e, place, :] for e in range(SECTIONS)], axis=1)
        right = jnp.concatenate([col[final, e, span, :] for e in range(SECTIONS)]
                                + [other_col[e, span, :] for e in range(SECTIONS)], axis=1)
        acc[core, place, :] += lax.dot_general(
            left, right, (((1,), (1,)), ((), ())), preferred_element_type=jnp.float32)
        return 0

    lax.fori_loop(first_half, 2, last, 0)

    def settle(f, _):
        trade(f).wait_recv()
        first = lax.rem(b + f, 2) * (tiles // 2)

        def finish(t, _):
            tile_row = first + t
            place = pl.ds(pl.multiple_of(tile_row * TILE, TILE), TILE)
            for c in range(width // TILE):
                span = pl.ds(c * TILE, TILE)
                keep = mask_ref[c, tile_row].astype(jnp.float32)
                out_ref[place, span] = (acc[core, place, span] + got[place, span]) * keep
            return 0

        lax.fori_loop(0, tiles // 2, finish, 0)
        trade(f).wait_send()
        return 0

    lax.fori_loop(0, 2, settle, 0)

    @pl.when(straight)
    def _():
        give_columns(2).wait_send()
        give_rows(1, 4).wait_send()

    @pl.when(jnp.logical_not(straight))
    def _():
        give_rows(0, 2).wait_send()
        give_rows(1, 3).wait_send()
        give_columns(4).wait_send()

    part = row_part(0, 0, 0)
    whole = row_half(0, 0)
    for n in range(3):
        send(whole, whole, zs.at[0, n], zr.at[0, 0], dev_x_up).wait_send()
        for way in range(2):
            due, one = pass_along_z(n + 1, way)

            @pl.when(due)
            def _():
                one.wait_send()

    def drain_x(i, _):
        for way in range(2):
            for n in range(3):
                send(part, part, xs.at[way, i, n], xr.at[0, 0, 0], dev_x_up).wait_send()
        return 0

    lax.fori_loop(0, 8, drain_x, 0)

    @pl.when(straight)
    def _():
        def drain(n, _):
            for q in range(2):
                hops = ring if q == 0 else lax.rem(4 - ring, 4)

                @pl.when(hops < 3)
                def _():
                    send(part, part, ys.at[q, n, 0], xr.at[0, 0, 0], dev_x_up).wait_send()
            return 0

        lax.fori_loop(0, 16, drain, 0)

    @pl.when(jnp.logical_not(straight))
    def _():
        def drain(j, _):
            for way in range(2):
                for n in range(4):
                    done = (n < 2) | ((n == 2) & ((ring != 0) | (j >= RELIEVED)))

                    @pl.when(done | ((n == 3) & (ring == 2) & (j < RELIEVED)))
                    def _():
                        send(part, part, ys.at[way, j, n], xr.at[0, 0, 0], dev_x_up).wait_send()
            for n in range(8):
                @pl.when((ring == 0) | (n >= 6) | ((n == 0) & (ring != 2)))
                def _():
                    send(part, part, cs.at[j, n], xr.at[0, 0, 0], dev_x_up).wait_send()
            return 0

        lax.fori_loop(0, 4, drain, 0)


def shards(a_values, a_pattern, c_mask):
    rows, depth = a_values.shape[1], a_values.shape[2]
    out_width = c_mask.shape[1] * TILE
    half = rows // 2
    vmem = pl.BlockSpec(memory_space=pltpu.VMEM)
    dma = pltpu.SemaphoreType.DMA
    return pl.pallas_call(
        functools.partial(kernel, rows),
        out_shape=jax.ShapeDtypeStruct((rows, out_width), jnp.float32),
        in_specs=[pl.BlockSpec(memory_space=pl.ANY)] * 3,
        out_specs=vmem,
        scratch_shapes=[
            pltpu.SMEM((SECTIONS, 1, rows // TILE), jnp.int32),
            pltpu.SMEM((c_mask.shape[1], rows // TILE), jnp.int32),
            pltpu.VMEM((16, SECTIONS, rows, depth), jnp.bfloat16),
            pltpu.VMEM((16, SECTIONS, half, depth), jnp.bfloat16),
            pltpu.VMEM((2, rows, out_width), jnp.float32),
            pltpu.VMEM((rows, out_width), jnp.float32),
            pltpu.VMEM((4, 2, SECTIONS, half // 2, depth), jnp.bfloat16),
            pltpu.VMEM((4, SECTIONS, half // 2, depth), jnp.bfloat16),
            pltpu.VMEM((SECTIONS, rows, depth), jnp.bfloat16),
            pltpu.VMEM((SECTIONS, half, depth), jnp.bfloat16),
            dma((3, 3)), dma((4, 2)), dma((2, 8, 3)), dma((16, 2, 2)),
            dma((2, 16, 4)), dma((16, 2)), dma((4, 8)), dma((4, 2)), dma((4,)), dma((5,)), dma((5,)), dma((3,)),
        ],
        compiler_params=pltpu.CompilerParams(
            collective_id=0, has_side_effects=True, vmem_limit_bytes=48 << 20),
        cost_estimate=pl.CostEstimate(
            flops=2 * rows * half * 16 * SECTIONS * depth, bytes_accessed=4 * rows * out_width, transcendentals=0),
        name="gather_and_multiply",
    )(a_values, a_pattern.transpose(0, 2, 1), c_mask.T)


def solution(mesh):
    return jax.shard_map(
        shards,
        mesh=mesh,
        in_specs=(P(None, "row", "col"), P(None, "row", "col"), P("row", "col")),
        out_specs=P("row", "col"),
        check_vma=False,
    )
```

```python
import functools

import jax
import jax.numpy as jnp
from jax import lax
from jax.experimental import pallas as pl
from jax.experimental.pallas import tpu as pltpu
from jax.sharding import PartitionSpec as P

TILE = 128
SECTIONS = 2
MESH = pl.DeviceIdType.MESH
START_Y = 2
EARLY_SCATTER, SCATTER, PASS_ON = (1, 3), (3, 3), (2, 4)
CROSS = (4, 4, 4)
GATHER = (8, 9, 8)
FORWARD, FORWARD_ROOT, FORWARD_OPPOSITE = 10, 11, 10
FINAL = 13
RELIEVED = 2
EARLY_Z = (0, 1)
LATE_Z = (8, 11, 14)
LAST_TICK = 24


def kernel(rows, a_ref, pat_hbm, mask_hbm, out_ref, pat_ref, mask_ref, row, col, acc, got, relay, transit, other_row, other_col,
           zs, zr, xs, xr, ys, cr, cs, rr, tr, es, er, ls):
    half, quarter = rows // 2, rows // 4
    width = half // 2
    tiles = rows // TILE

    row_id, col_id = lax.axis_index("row"), lax.axis_index("col")
    y, h = lax.div(row_id, 2), lax.rem(row_id, 2)
    x, zl, core = lax.div(col_id, 8), lax.rem(lax.div(col_id, 2), 4), lax.rem(col_id, 2)
    a, b = lax.div(zl, 2), lax.rem(zl, 2)
    x_up, x_down, x_far = lax.rem(x + 1, 4), lax.rem(x + 3, 4), lax.rem(x + 2, 4)
    ring = lax.rem(y - x + 4, 4)
    straight = h == a

    def device(x=x, y=y, h=h, zl=zl, core=core):
        return (y * 2 + h, x * 8 + zl * 2 + core)

    dev_x_up, dev_x_down = device(x=x_up), device(x=x_down)
    dev_y_up, dev_y_down = device(y=lax.rem(y + 1, 4)), device(y=lax.rem(y + 3, 4))
    dev_over, dev_core = device(h=1 - h, zl=2 * (1 - a) + b), device(core=1 - core)
    z_peers = [2 * lax.rem(a + k // 2, 2) + lax.rem(b + k % 2, 2) for k in (1, 2, 3)]
    partners = [dev_x_up, dev_x_down, dev_y_up, dev_y_down, dev_over, dev_core]
    partners += [device(zl=z) for z in z_peers]

    barrier = pltpu.get_barrier_semaphore()
    for partner in partners:
        pl.semaphore_signal(barrier, inc=1, device_id=partner, device_id_type=MESH)

    own = x * 4 + zl

    def own_half(g):
        return pl.ds(pl.multiple_of(g * half, half), half)

    loads = [pltpu.make_async_copy(pat_hbm, pat_ref, ls.at[0])]
    for n in range(2):
        place = own_half(lax.rem(b + n, 2))
        loads.append(pltpu.make_async_copy(a_ref.at[:, place, :], row.at[own, :, place, :], ls.at[1 + n]))
    loads.append(pltpu.make_async_copy(mask_hbm, mask_ref, ls.at[3]))
    for load in loads:
        load.start()

    def mask_half(g):
        for t in range(tiles // 2):
            place = pl.ds(pl.multiple_of(g * half + t * TILE, TILE), TILE)
            for section in range(SECTIONS):
                keep = pat_ref[section, 0, g * (tiles // 2) + t].astype(jnp.float32)
                tile = row[own, section, place, :].astype(jnp.float32) * keep
                row[own, section, place, :] = tile.astype(jnp.bfloat16)

    loads[0].wait()
    loads[1].wait()
    mask_half(b)
    pl.semaphore_wait(barrier, len(partners))

    def send(src, dst, send_sem, recv_sem, target):
        return pltpu.make_async_remote_copy(
            src_ref=src, dst_ref=dst, send_sem=send_sem, recv_sem=recv_sem,
            device_id=target, device_id_type=MESH)

    def row_half(s, g):
        return row.at[s, :, pl.ds(pl.multiple_of(g * half, half), half), :]

    def row_part(s, g, q):
        return row.at[s, :, pl.ds(pl.multiple_of(g * half + q * quarter, quarter), quarter), :]

    def col_part(s, q):
        return col.at[s, :, pl.ds(pl.multiple_of(q * quarter, quarter), quarter), :]

    def z_of(k, first=a):
        return 2 * lax.rem(first + lax.div(k, 2), 2) + lax.rem(b + lax.rem(k, 2), 2)

    def item(i):
        k = lax.rem(i, 4)
        return k, z_of(k), lax.rem(b + lax.div(i, 4), 2)

    def wait_row(s, g, q):
        ref = row_part(s, g, q)
        send(ref, ref, xs.at[0, 0, 0], xr.at[s, g, q], dev_x_up).wait_recv()

    def wait_col(s, q):
        ref = col_part(s, q)
        send(ref, ref, xs.at[0, 0, 0], cr.at[s, q], dev_y_up).wait_recv()

    def send_item(i):
        _, z, g = item(i)
        s = x * 4 + z
        for n, (way, q, target) in enumerate(
                ((0, 0, dev_x_up), (1, 1, dev_x_down), (0, 1, dev_x_up), (1, 0, dev_x_down))):
            ref = row_part(s, g, q)
            send(ref, ref, xs.at[way, i, n // 2], xr.at[s, g, q], target).start()

    send_item(jnp.int32(0))
    loads[2].wait()
    mask_half(1 - b)
    loads[3].wait()

    def send_along_z(n):
        g = lax.rem(z_peers[n], 2)
        ref = row_half(own, g)
        send(ref, ref, zs.at[0, n], zr.at[zl, g], device(zl=z_peers[n])).start()

    send_along_z(0)

    def pass_along_z(k, way):
        to = zl + 1 - 2 * way
        block = 2 * lax.rem(lax.div(to + 4, 2) + k // 2, 2) + lax.rem(to + 4 + k % 2, 2)
        due = (to >= 0) & (to < 4) & ((block <= zl) if way == 0 else (block >= zl))
        ref = row_half(x * 4 + block, b)
        return due, send(ref, ref, zs.at[1 + way, k - 1], zr.at[block, b], device(zl=lax.rem(to + 4, 4)))
    acc[...] = jnp.zeros_like(acc)

    def slice_of(n, first=h):
        o = lax.rem(n, 4)
        step = jnp.where(o == 0, 0, jnp.where(o == 1, 3, jnp.where(o == 2, 1, 2)))
        return lax.rem(x + step, 4) * 4 + z_of(lax.div(n, 4), first)

    def crossing(j, r, first=h):
        o = jnp.where(r == 0, 3, jnp.where(r == 2, 0, lax.div(r + 1, 2)))
        return slice_of(4 * j + o, first)

    def accumulate(slices, f):
        place = pl.ds(pl.multiple_of(lax.rem(b + f, 2) * half, half), half)
        left = jnp.concatenate([row[s, e, place, :] for s in slices for e in range(SECTIONS)], axis=1)
        right = jnp.concatenate([col[s, e] for s in slices for e in range(SECTIONS)], axis=1)
        total = lax.dot_general(left, right, (((1,), (1,)), ((), ())), preferred_element_type=jnp.float32)
        for side in range(2):
            acc[side, place, :] += total[:, side * width:(side + 1) * width]

    def group_slices(group):
        return [slice_of(group * 4 + o) for o in range(4)]

    r_down, r_up, r_far = lax.rem(ring + 3, 4), lax.rem(ring + 1, 4), lax.rem(ring + 2, 4)

    def wait_near_rows(i):
        _, z, g = item(i)
        wait_row(x_down * 4 + z, g, 1)
        wait_row(x_up * 4 + z, g, 0)

    def wait_far_rows(i):
        _, z, g = item(i)
        wait_row(x_far * 4 + z, g, 0)
        wait_row(x_far * 4 + z, g, 1)

    def wait_near_columns(j):
        for way, r in ((0, r_down), (1, r_up)):
            wait_col(crossing(j, r), 1 - way)

    def wait_far_columns(j):
        for q in range(2):
            wait_col(crossing(j, r_far), q)

    def scatter(j, jobs):
        for n, r, q, dst, recv_sem, target in jobs:
            send(row_part(crossing(j, r, a), b, q), dst, cs.at[j, n], recv_sem, target).start()

    def scatter_near(j):
        jobs = []
        for q in range(2):
            jobs.append((2 + q, 1, q, relay.at[j, q], rr.at[j, q], dev_y_up))
            jobs.append((4 + q, 3, q, relay.at[j, q], rr.at[j, q], dev_y_down))
        scatter(j, jobs)

    scatters = jnp.logical_not(straight) & (ring == 0)

    def tick(m, _):
        i, sub = lax.div(m, 3), lax.rem(m, 3)

        @pl.when((sub == 0) & (i >= 1))
        def _():
            wait_near_rows(i - 1)

            @pl.when(scatters & (i <= 4))
            def _():
                scatter_near(i - 1)

            wait_far_rows(i - 1)

        @pl.when((sub == 1) & (i < 8))
        def _():
            _, z, g = item(i)
            for way, q, source, target in ((0, 0, x_down, dev_x_up), (1, 1, x_up, dev_x_down)):
                s = source * 4 + z
                wait_row(s, g, q)
                ref = row_part(s, g, q)
                send(ref, ref, xs.at[way, i, 2], xr.at[s, g, q], target).start()

        @pl.when((sub == 2) & (i < 7))
        def _():
            k, z, g = item(i + 1)

            @pl.when(k != 0)
            def _():
                ref = row_half(x * 4 + z, g)
                send(ref, ref, xs.at[0, 0, 0], zr.at[z, g], dev_x_up).wait_recv()

            send_item(i + 1)

        for n in (1, 2):
            @pl.when(m == EARLY_Z[n - 1])
            def _():
                send_along_z(n)

        for k in (1, 2, 3):
            for way in range(2):
                due, one = pass_along_z(k, way)

                @pl.when(due & (m == LATE_Z[k - 1]))
                def _():
                    one.start()

        @pl.when(straight)
        def _():
            @pl.when((ring == 0) & (m >= START_Y) & (m < START_Y + 16))
            def _():
                s = slice_of(m - START_Y)
                col[s] = row[s, :, pl.ds(pl.multiple_of(b * half, half), half), :]
                for q, target in ((0, dev_y_up), (1, dev_y_down)):
                    send(row_part(s, b, q), col_part(s, q), ys.at[q, m - START_Y, 0], cr.at[s, q], target).start()

            for q, target in ((0, dev_y_up), (1, dev_y_down)):
                hops = ring if q == 0 else 4 - ring
                n = m - START_Y - 2 * hops

                @pl.when((ring != 0) & (n >= 0) & (n < 16))
                def _():
                    s = slice_of(n)
                    wait_col(s, q)

                    @pl.when(hops < 3)
                    def _():
                        ref = col_part(s, q)
                        send(ref, ref, ys.at[q, n, 0], cr.at[s, q], target).start()

        @pl.when(jnp.logical_not(straight))
        def _():
            def at(when):
                first, step = when if isinstance(when, tuple) else (when, 4)
                since = m - first + 4 * step
                here = (m >= first) & (m < first + 4 * step) & (lax.rem(since, step) == 0)
                return here, lax.div(since, step) - 4

            def by_place(ticks):
                return jnp.where(ring == 0, ticks[0], jnp.where(ring == 2, ticks[2], ticks[1]))

            beside = lax.rem(ring, 2) == 1

            here, j = at(EARLY_SCATTER)

            @pl.when((ring == 0) & here)
            def _():
                scatter(j, ((0, 2, 0, transit.at[j], tr.at[j], dev_y_up),
                            (1, 2, 1, transit.at[j], tr.at[j], dev_y_down)))

            here, j = at(SCATTER)

            @pl.when((ring == 0) & here)
            def _():
                jobs = []
                s = crossing(j, 0, a)
                for q in range(2):
                    jobs.append((6 + q, 0, q, col_part(s, q), cr.at[s, q], dev_over))
                scatter(j, jobs)

            here, j = at(PASS_ON)

            @pl.when(beside & here)
            def _():
                send(transit.at[j], transit.at[j], cs.at[j, 0], tr.at[j], dev_y_up).wait_recv()

                @pl.when(ring == 1)
                def _():
                    send(transit.at[j], relay.at[j, 0], cs.at[j, 0], rr.at[j, 0], dev_y_up).start()

                @pl.when(ring == 3)
                def _():
                    send(transit.at[j], relay.at[j, 1], cs.at[j, 0], rr.at[j, 1], dev_y_down).start()

            here, j = at(by_place(CROSS))

            @pl.when((ring != 0) & here)
            def _():
                s = crossing(j, ring, a)
                for q in range(2):
                    ref = relay.at[j, q]
                    send(ref, ref, cs.at[j, 6 + q], rr.at[j, q], dev_over).wait_recv()
                    send(ref, col_part(s, q), cs.at[j, 6 + q], cr.at[s, q], dev_over).start()

            here, j = at(by_place(GATHER))

            @pl.when(here)
            def _():
                s = crossing(j, ring)
                for q in range(2):
                    wait_col(s, q)
                for n, (way, q, target) in enumerate(
                        ((0, 0, dev_y_up), (1, 1, dev_y_down), (0, 1, dev_y_up), (1, 0, dev_y_down))):
                    ref = col_part(s, q)
                    send(ref, ref, ys.at[way, j, n // 2], cr.at[s, q], target).start()

            for way, r, target in ((0, r_down, dev_y_up), (1, r_up, dev_y_down)):
                here, j = at(jnp.where(beside, jnp.where(r == 0, FORWARD_ROOT, FORWARD_OPPOSITE), FORWARD))

                @pl.when(here)
                def _():
                    s = crossing(j, r)
                    wait_col(s, way)

                    @pl.when((ring != 0) | (j >= RELIEVED))
                    def _():
                        ref = col_part(s, way)
                        send(ref, ref, ys.at[way, j, 2], cr.at[s, way], target).start()

                    @pl.when((ring == 2) & (j < RELIEVED))
                    def _():
                        wait_col(s, 1 - way)
                        ref = col_part(s, 1 - way)
                        send(ref, ref, ys.at[way, j, 3], cr.at[s, 1 - way], target).start()

            here, j = at(FINAL)

            @pl.when(here)
            def _():
                @pl.when((ring != 2) | (j >= RELIEVED))
                def _():
                    wait_near_columns(j)

                wait_far_columns(j)

        start = jnp.where(straight, 12, FINAL + 1)
        first_due = (m >= start) & (m < start + 12) & (lax.rem(m + 16 - start, 4) == 0)
        second_due = jnp.where(straight, (m >= 15) & (m < 24) & (sub == 0), (m == 21) | (m == 23))
        second = jnp.where(straight, i - 5, jnp.where(m == 21, 0, 2))

        def product(f, _):
            @pl.when(jnp.where(f == 0, first_due, second_due))
            def _():
                accumulate(group_slices(jnp.where(f == 0, lax.div(m + 16 - start, 4) - 4, second)), f)
            return 0

        lax.fori_loop(0, 2, product, 0)
        return 0

    lax.fori_loop(0, LAST_TICK, tick, 0)

    def trade(f):
        g = lax.rem(b + f, 2)
        place = pl.ds(pl.multiple_of(g * half, half), half)
        return send(acc.at[1 - core, place, :], got.at[place, :], es.at[f], er.at[f], dev_core)

    @pl.when(jnp.logical_not(straight))
    def _():
        wait_near_rows(7)
        wait_far_rows(7)

    ends = [jnp.where(straight, slice_of(12 + o), crossing(3, lax.rem(ring + turn, 4)))
            for o, turn in ((0, 0), (1, 3), (2, 1), (3, 2))]
    final = ends[3]

    def half_place(f):
        return pl.ds(pl.multiple_of(lax.rem(b + f, 2) * half, half), half)

    def give_rows(f, n):
        place = half_place(f)
        return send(row.at[final, :, place, :], other_row.at[:, place, :], es.at[n], er.at[n], dev_core)

    def give_columns(n):
        return send(col.at[final], other_col, es.at[n], er.at[n], dev_core)

    @pl.when(straight)
    def _():
        give_columns(2).start()

    @pl.when(jnp.logical_not(straight))
    def _():
        give_rows(0, 2).start()
        give_rows(1, 3).start()

    accumulate([jnp.where(straight, p, q) for p, q in zip(group_slices(3), group_slices(1))], jnp.where(straight, 0, 1))

    @pl.when(straight)
    def _():
        trade(0).start()
        wait_near_rows(7)

    @pl.when(jnp.logical_not(straight))
    def _():
        wait_near_columns(3)

    first_half = jnp.where(straight, 1, 0)

    def nearly(f, _):
        accumulate(ends[:3], f)
        trade(f).start()
        return 0

    lax.fori_loop(first_half, 2, nearly, 0)

    @pl.when(straight)
    def _():
        wait_far_rows(7)
        give_rows(1, 4).start()
        give_columns(2).wait_recv()
        give_rows(1, 4).wait_recv()

    @pl.when(jnp.logical_not(straight))
    def _():
        wait_far_columns(3)
        give_columns(4).start()
        give_rows(0, 2).wait_recv()
        give_rows(1, 3).wait_recv()
        give_columns(4).wait_recv()

    def last(f, _):
        place = half_place(f)
        span = pl.ds(pl.multiple_of(core * width, width), width)
        left = jnp.concatenate([row[final, e, place, :] for e in range(SECTIONS)]
                               + [other_row[e, place, :] for e in range(SECTIONS)], axis=1)
        right = jnp.concatenate([col[final, e, span, :] for e in range(SECTIONS)]
                                + [other_col[e, span, :] for e in range(SECTIONS)], axis=1)
        acc[core, place, :] += lax.dot_general(
            left, right, (((1,), (1,)), ((), ())), preferred_element_type=jnp.float32)
        return 0

    lax.fori_loop(first_half, 2, last, 0)

    def settle(f, _):
        trade(f).wait_recv()
        first = lax.rem(b + f, 2) * (tiles // 2)

        def finish(t, _):
            tile_row = first + t
            place = pl.ds(pl.multiple_of(tile_row * TILE, TILE), TILE)
            for c in range(width // TILE):
                span = pl.ds(c * TILE, TILE)
                keep = mask_ref[c, tile_row].astype(jnp.float32)
                out_ref[place, span] = (acc[core, place, span] + got[place, span]) * keep
            return 0

        lax.fori_loop(0, tiles // 2, finish, 0)
        trade(f).wait_send()
        return 0

    lax.fori_loop(0, 2, settle, 0)

    @pl.when(straight)
    def _():
        give_columns(2).wait_send()
        give_rows(1, 4).wait_send()

    @pl.when(jnp.logical_not(straight))
    def _():
        give_rows(0, 2).wait_send()
        give_rows(1, 3).wait_send()
        give_columns(4).wait_send()

    part = row_part(0, 0, 0)
    whole = row_half(0, 0)
    for n in range(3):
        send(whole, whole, zs.at[0, n], zr.at[0, 0], dev_x_up).wait_send()
        for way in range(2):
            due, one = pass_along_z(n + 1, way)

            @pl.when(due)
            def _():
                one.wait_send()

    def drain_x(i, _):
        for way in range(2):
            for n in range(3):
                send(part, part, xs.at[way, i, n], xr.at[0, 0, 0], dev_x_up).wait_send()
        return 0

    lax.fori_loop(0, 8, drain_x, 0)

    @pl.when(straight)
    def _():
        def drain(n, _):
            for q in range(2):
                hops = ring if q == 0 else lax.rem(4 - ring, 4)

                @pl.when(hops < 3)
                def _():
                    send(part, part, ys.at[q, n, 0], xr.at[0, 0, 0], dev_x_up).wait_send()
            return 0

        lax.fori_loop(0, 16, drain, 0)

    @pl.when(jnp.logical_not(straight))
    def _():
        def drain(j, _):
            for way in range(2):
                for n in range(4):
                    done = (n < 2) | ((n == 2) & ((ring != 0) | (j >= RELIEVED)))

                    @pl.when(done | ((n == 3) & (ring == 2) & (j < RELIEVED)))
                    def _():
                        send(part, part, ys.at[way, j, n], xr.at[0, 0, 0], dev_x_up).wait_send()
            for n in range(8):
                @pl.when((ring == 0) | (n >= 6) | ((n == 0) & (ring != 2)))
                def _():
                    send(part, part, cs.at[j, n], xr.at[0, 0, 0], dev_x_up).wait_send()
            return 0

        lax.fori_loop(0, 4, drain, 0)


def shards(a_values, a_pattern, c_mask):
    rows, depth = a_values.shape[1], a_values.shape[2]
    out_width = c_mask.shape[1] * TILE
    half = rows // 2
    vmem = pl.BlockSpec(memory_space=pltpu.VMEM)
    dma = pltpu.SemaphoreType.DMA
    return pl.pallas_call(
        functools.partial(kernel, rows),
        out_shape=jax.ShapeDtypeStruct((rows, out_width), jnp.float32),
        in_specs=[pl.BlockSpec(memory_space=pl.ANY)] * 3,
        out_specs=vmem,
        scratch_shapes=[
            pltpu.SMEM((SECTIONS, 1, rows // TILE), jnp.int32),
            pltpu.SMEM((c_mask.shape[1], rows // TILE), jnp.int32),
            pltpu.VMEM((16, SECTIONS, rows, depth), jnp.bfloat16),
            pltpu.VMEM((16, SECTIONS, half, depth), jnp.bfloat16),
            pltpu.VMEM((2, rows, out_width), jnp.float32),
            pltpu.VMEM((rows, out_width), jnp.float32),
            pltpu.VMEM((4, 2, SECTIONS, half // 2, depth), jnp.bfloat16),
            pltpu.VMEM((4, SECTIONS, half // 2, depth), jnp.bfloat16),
            pltpu.VMEM((SECTIONS, rows, depth), jnp.bfloat16),
            pltpu.VMEM((SECTIONS, half, depth), jnp.bfloat16),
            dma((3, 3)), dma((4, 2)), dma((2, 8, 3)), dma((16, 2, 2)),
            dma((2, 16, 4)), dma((16, 2)), dma((4, 8)), dma((4, 2)), dma((4,)), dma((5,)), dma((5,)), dma((4,)),
        ],
        compiler_params=pltpu.CompilerParams(
            collective_id=0, has_side_effects=True, vmem_limit_bytes=48 << 20),
        cost_estimate=pl.CostEstimate(
            flops=2 * rows * half * 16 * SECTIONS * depth, bytes_accessed=4 * rows * out_width, transcendentals=0),
        name="gather_and_multiply",
    )(a_values, a_pattern.transpose(0, 2, 1), c_mask.T)


def solution(mesh):
    return jax.shard_map(
        shards,
        mesh=mesh,
        in_specs=(P(None, "row", "col"), P(None, "row", "col"), P("row", "col")),
        out_specs=P("row", "col"),
        check_vma=False,
    )
```

```python
import functools

import jax
import jax.numpy as jnp
from jax import lax
from jax.experimental import pallas as pl
from jax.experimental.pallas import tpu as pltpu
from jax.sharding import PartitionSpec as P

TILE = 128
SECTIONS = 2
MESH = pl.DeviceIdType.MESH
START_Y = 2
EARLY_SCATTER, SCATTER, PASS_ON = (1, 3), (3, 3), (2, 4)
CROSS = (4, 4, 4)
GATHER = (8, 9, 8)
FORWARD, FORWARD_ROOT, FORWARD_OPPOSITE = 10, 11, 10
FINAL = 13
RELIEVED = 2
EARLY_Z = (0, 1)
LATE_Z = (8, 11, 14)
LAST_TICK = 24


def kernel(rows, a_ref, pat_hbm, mask_hbm, out_ref, pat_ref, mask_ref, row, col, acc, got, relay, transit, other_row, other_col,
           zs, zr, xs, xr, ys, cr, cs, rr, tr, es, er, ls):
    half, quarter = rows // 2, rows // 4
    width = half // 2
    tiles = rows // TILE

    row_id, col_id = lax.axis_index("row"), lax.axis_index("col")
    y, h = lax.div(row_id, 2), lax.rem(row_id, 2)
    x, zl, core = lax.div(col_id, 8), lax.rem(lax.div(col_id, 2), 4), lax.rem(col_id, 2)
    a, b = lax.div(zl, 2), lax.rem(zl, 2)
    x_up, x_down, x_far = lax.rem(x + 1, 4), lax.rem(x + 3, 4), lax.rem(x + 2, 4)
    ring = lax.rem(y - x + 4, 4)
    straight = h == a

    def device(x=x, y=y, h=h, zl=zl, core=core):
        return (y * 2 + h, x * 8 + zl * 2 + core)

    dev_x_up, dev_x_down = device(x=x_up), device(x=x_down)
    dev_y_up, dev_y_down = device(y=lax.rem(y + 1, 4)), device(y=lax.rem(y + 3, 4))
    dev_over, dev_core = device(h=1 - h, zl=2 * (1 - a) + b), device(core=1 - core)
    z_peers = [2 * lax.rem(a + k // 2, 2) + lax.rem(b + k % 2, 2) for k in (1, 2, 3)]
    partners = [dev_x_up, dev_x_down, dev_y_up, dev_y_down, dev_over, dev_core]
    partners += [device(zl=z) for z in z_peers]

    barrier = pltpu.get_barrier_semaphore()
    for partner in partners:
        pl.semaphore_signal(barrier, inc=1, device_id=partner, device_id_type=MESH)

    own = x * 4 + zl

    def own_half(g):
        return pl.ds(pl.multiple_of(g * half, half), half)

    loads = [pltpu.make_async_copy(pat_hbm, pat_ref, ls.at[0])]
    for n in range(2):
        place = own_half(lax.rem(b + n, 2))
        loads.append(pltpu.make_async_copy(a_ref.at[:, place, :], row.at[own, :, place, :], ls.at[1 + n]))
    loads.append(pltpu.make_async_copy(mask_hbm, mask_ref, ls.at[3]))
    for load in loads:
        load.start()

    def mask_half(g):
        for t in range(tiles // 2):
            place = pl.ds(pl.multiple_of(g * half + t * TILE, TILE), TILE)
            for section in range(SECTIONS):
                keep = pat_ref[section, 0, g * (tiles // 2) + t].astype(jnp.float32)
                tile = row[own, section, place, :].astype(jnp.float32) * keep
                row[own, section, place, :] = tile.astype(jnp.bfloat16)

    loads[0].wait()
    loads[1].wait()
    mask_half(b)
    pl.semaphore_wait(barrier, len(partners))

    def send(src, dst, send_sem, recv_sem, target):
        return pltpu.make_async_remote_copy(
            src_ref=src, dst_ref=dst, send_sem=send_sem, recv_sem=recv_sem,
            device_id=target, device_id_type=MESH)

    def row_half(s, g):
        return row.at[s, :, pl.ds(pl.multiple_of(g * half, half), half), :]

    def row_part(s, g, q):
        return row.at[s, :, pl.ds(pl.multiple_of(g * half + q * quarter, quarter), quarter), :]

    def col_part(s, q):
        return col.at[s, :, pl.ds(pl.multiple_of(q * quarter, quarter), quarter), :]

    def z_of(k, first=a):
        return 2 * lax.rem(first + lax.div(k, 2), 2) + lax.rem(b + lax.rem(k, 2), 2)

    def item(i):
        k = lax.rem(i, 4)
        return k, z_of(k), lax.rem(b + lax.div(i, 4), 2)

    def wait_row(s, g, q):
        ref = row_part(s, g, q)
        send(ref, ref, xs.at[0, 0, 0], xr.at[s, g, q], dev_x_up).wait_recv()

    def wait_col(s, q):
        ref = col_part(s, q)
        send(ref, ref, xs.at[0, 0, 0], cr.at[s, q], dev_y_up).wait_recv()

    def send_item(i):
        _, z, g = item(i)
        s = x * 4 + z
        for n, (way, q, target) in enumerate(
                ((0, 0, dev_x_up), (1, 1, dev_x_down), (0, 1, dev_x_up), (1, 0, dev_x_down))):
            ref = row_part(s, g, q)
            send(ref, ref, xs.at[way, i, n // 2], xr.at[s, g, q], target).start()

    send_item(jnp.int32(0))
    loads[2].wait()
    mask_half(1 - b)
    loads[3].wait()

    def send_along_z(n):
        g = lax.rem(z_peers[n], 2)
        ref = row_half(own, g)
        send(ref, ref, zs.at[0, n], zr.at[zl, g], device(zl=z_peers[n])).start()

    send_along_z(0)

    def pass_along_z(k, way):
        to = zl + 1 - 2 * way
        block = 2 * lax.rem(lax.div(to + 4, 2) + k // 2, 2) + lax.rem(to + 4 + k % 2, 2)
        due = (to >= 0) & (to < 4) & ((block <= zl) if way == 0 else (block >= zl))
        ref = row_half(x * 4 + block, b)
        return due, send(ref, ref, zs.at[1 + way, k - 1], zr.at[block, b], device(zl=lax.rem(to + 4, 4)))
    acc[...] = jnp.zeros_like(acc)

    def slice_of(n, first=h):
        o = lax.rem(n, 4)
        step = jnp.where(o == 0, 0, jnp.where(o == 1, 3, jnp.where(o == 2, 1, 2)))
        return lax.rem(x + step, 4) * 4 + z_of(lax.div(n, 4), first)

    def crossing(j, r, first=h):
        o = jnp.where(r == 0, 3, jnp.where(r == 2, 0, lax.div(r + 1, 2)))
        return slice_of(4 * j + o, first)

    def accumulate(slices, f):
        place = pl.ds(pl.multiple_of(lax.rem(b + f, 2) * half, half), half)
        left = jnp.concatenate([row[s, e, place, :] for s in slices for e in range(SECTIONS)], axis=1)
        right = jnp.concatenate([col[s, e] for s in slices for e in range(SECTIONS)], axis=1)
        total = lax.dot_general(left, right, (((1,), (1,)), ((), ())), preferred_element_type=jnp.float32)
        for side in range(2):
            acc[side, place, :] += total[:, side * width:(side + 1) * width]

    def group_slices(group):
        return [slice_of(group * 4 + o) for o in range(4)]

    r_down, r_up, r_far = lax.rem(ring + 3, 4), lax.rem(ring + 1, 4), lax.rem(ring + 2, 4)

    def wait_near_rows(i):
        _, z, g = item(i)
        wait_row(x_down * 4 + z, g, 1)
        wait_row(x_up * 4 + z, g, 0)

    def wait_far_rows(i):
        _, z, g = item(i)
        wait_row(x_far * 4 + z, g, 0)
        wait_row(x_far * 4 + z, g, 1)

    def wait_near_columns(j):
        for way, r in ((0, r_down), (1, r_up)):
            wait_col(crossing(j, r), 1 - way)

    def wait_far_columns(j):
        for q in range(2):
            wait_col(crossing(j, r_far), q)

    def scatter(j, jobs):
        for n, r, q, dst, recv_sem, target in jobs:
            send(row_part(crossing(j, r, a), b, q), dst, cs.at[j, n], recv_sem, target).start()

    def scatter_near(j):
        jobs = []
        for q in range(2):
            jobs.append((2 + q, 1, q, relay.at[j, q], rr.at[j, q], dev_y_up))
            jobs.append((4 + q, 3, q, relay.at[j, q], rr.at[j, q], dev_y_down))
        scatter(j, jobs)

    scatters = jnp.logical_not(straight) & (ring == 0)

    def tick(m, _):
        i, sub = lax.div(m, 3), lax.rem(m, 3)

        @pl.when((sub == 0) & (i >= 1))
        def _():
            wait_near_rows(i - 1)

            @pl.when(scatters & (i <= 4))
            def _():
                scatter_near(i - 1)

            @pl.when(scatters | (i > 4))
            def _():
                wait_far_rows(i - 1)

        @pl.when((sub == 1) & (i < 8))
        def _():
            _, z, g = item(i)
            for way, q, source, target in ((0, 0, x_down, dev_x_up), (1, 1, x_up, dev_x_down)):
                s = source * 4 + z
                wait_row(s, g, q)
                ref = row_part(s, g, q)
                send(ref, ref, xs.at[way, i, 2], xr.at[s, g, q], target).start()

            @pl.when(jnp.logical_not(scatters) & (i >= 1) & (i <= 4))
            def _():
                wait_far_rows(i - 1)

        @pl.when((sub == 2) & (i < 7))
        def _():
            k, z, g = item(i + 1)

            @pl.when(k != 0)
            def _():
                ref = row_half(x * 4 + z, g)
                send(ref, ref, xs.at[0, 0, 0], zr.at[z, g], dev_x_up).wait_recv()

            send_item(i + 1)

        for n in (1, 2):
            @pl.when(m == EARLY_Z[n - 1])
            def _():
                send_along_z(n)

        for k in (1, 2, 3):
            for way in range(2):
                due, one = pass_along_z(k, way)

                @pl.when(due & (m == LATE_Z[k - 1]))
                def _():
                    one.start()

        @pl.when(straight)
        def _():
            @pl.when((ring == 0) & (m >= START_Y) & (m < START_Y + 16))
            def _():
                s = slice_of(m - START_Y)
                col[s] = row[s, :, pl.ds(pl.multiple_of(b * half, half), half), :]
                for q, target in ((0, dev_y_up), (1, dev_y_down)):
                    send(row_part(s, b, q), col_part(s, q), ys.at[q, m - START_Y, 0], cr.at[s, q], target).start()

            for q, target in ((0, dev_y_up), (1, dev_y_down)):
                hops = ring if q == 0 else 4 - ring
                n = m - START_Y - 2 * hops

                @pl.when((ring != 0) & (n >= 0) & (n < 16))
                def _():
                    s = slice_of(n)
                    wait_col(s, q)

                    @pl.when(hops < 3)
                    def _():
                        ref = col_part(s, q)
                        send(ref, ref, ys.at[q, n, 0], cr.at[s, q], target).start()

        @pl.when(jnp.logical_not(straight))
        def _():
            def at(when):
                first, step = when if isinstance(when, tuple) else (when, 4)
                since = m - first + 4 * step
                here = (m >= first) & (m < first + 4 * step) & (lax.rem(since, step) == 0)
                return here, lax.div(since, step) - 4

            def by_place(ticks):
                return jnp.where(ring == 0, ticks[0], jnp.where(ring == 2, ticks[2], ticks[1]))

            beside = lax.rem(ring, 2) == 1

            here, j = at(EARLY_SCATTER)

            @pl.when((ring == 0) & here)
            def _():
                scatter(j, ((0, 2, 0, transit.at[j], tr.at[j], dev_y_up),
                            (1, 2, 1, transit.at[j], tr.at[j], dev_y_down)))

            here, j = at(SCATTER)

            @pl.when((ring == 0) & here)
            def _():
                jobs = []
                s = crossing(j, 0, a)
                for q in range(2):
                    jobs.append((6 + q, 0, q, col_part(s, q), cr.at[s, q], dev_over))
                scatter(j, jobs)

            here, j = at(PASS_ON)

            @pl.when(beside & here)
            def _():
                send(transit.at[j], transit.at[j], cs.at[j, 0], tr.at[j], dev_y_up).wait_recv()

                @pl.when(ring == 1)
                def _():
                    send(transit.at[j], relay.at[j, 0], cs.at[j, 0], rr.at[j, 0], dev_y_up).start()

                @pl.when(ring == 3)
                def _():
                    send(transit.at[j], relay.at[j, 1], cs.at[j, 0], rr.at[j, 1], dev_y_down).start()

            here, j = at(by_place(CROSS))

            @pl.when((ring != 0) & here)
            def _():
                s = crossing(j, ring, a)
                for q in range(2):
                    ref = relay.at[j, q]
                    send(ref, ref, cs.at[j, 6 + q], rr.at[j, q], dev_over).wait_recv()
                    send(ref, col_part(s, q), cs.at[j, 6 + q], cr.at[s, q], dev_over).start()

            here, j = at(by_place(GATHER))

            @pl.when(here)
            def _():
                s = crossing(j, ring)
                for q in range(2):
                    wait_col(s, q)
                for n, (way, q, target) in enumerate(
                        ((0, 0, dev_y_up), (1, 1, dev_y_down), (0, 1, dev_y_up), (1, 0, dev_y_down))):
                    ref = col_part(s, q)
                    send(ref, ref, ys.at[way, j, n // 2], cr.at[s, q], target).start()

            for way, r, target in ((0, r_down, dev_y_up), (1, r_up, dev_y_down)):
                here, j = at(jnp.where(beside, jnp.where(r == 0, FORWARD_ROOT, FORWARD_OPPOSITE), FORWARD))

                @pl.when(here)
                def _():
                    s = crossing(j, r)
                    wait_col(s, way)

                    @pl.when((ring != 0) | (j >= RELIEVED))
                    def _():
                        ref = col_part(s, way)
                        send(ref, ref, ys.at[way, j, 2], cr.at[s, way], target).start()

                    @pl.when((ring == 2) & (j < RELIEVED))
                    def _():
                        wait_col(s, 1 - way)
                        ref = col_part(s, 1 - way)
                        send(ref, ref, ys.at[way, j, 3], cr.at[s, 1 - way], target).start()

            here, j = at(FINAL)

            @pl.when(here)
            def _():
                @pl.when((ring != 2) | (j >= RELIEVED))
                def _():
                    wait_near_columns(j)

                wait_far_columns(j)

        start = jnp.where(straight, 12, FINAL + 1)
        first_due = (m >= start) & (m < start + 12) & (lax.rem(m + 16 - start, 4) == 0)
        second_due = jnp.where(straight, (m >= 15) & (m < 24) & (sub == 0), (m == 21) | (m == 23))
        second = jnp.where(straight, i - 5, jnp.where(m == 21, 0, 2))

        def product(f, _):
            @pl.when(jnp.where(f == 0, first_due, second_due))
            def _():
                accumulate(group_slices(jnp.where(f == 0, lax.div(m + 16 - start, 4) - 4, second)), f)
            return 0

        lax.fori_loop(0, 2, product, 0)
        return 0

    lax.fori_loop(0, LAST_TICK, tick, 0)

    def trade(f):
        g = lax.rem(b + f, 2)
        place = pl.ds(pl.multiple_of(g * half, half), half)
        return send(acc.at[1 - core, place, :], got.at[place, :], es.at[f], er.at[f], dev_core)

    @pl.when(jnp.logical_not(straight))
    def _():
        wait_near_rows(7)
        wait_far_rows(7)

    ends = [jnp.where(straight, slice_of(12 + o), crossing(3, lax.rem(ring + turn, 4)))
            for o, turn in ((0, 0), (1, 3), (2, 1), (3, 2))]
    final = ends[3]

    def half_place(f):
        return pl.ds(pl.multiple_of(lax.rem(b + f, 2) * half, half), half)

    def give_rows(f, n):
        place = half_place(f)
        return send(row.at[final, :, place, :], other_row.at[:, place, :], es.at[n], er.at[n], dev_core)

    def give_columns(n):
        return send(col.at[final], other_col, es.at[n], er.at[n], dev_core)

    @pl.when(straight)
    def _():
        give_columns(2).start()

    @pl.when(jnp.logical_not(straight))
    def _():
        give_rows(0, 2).start()
        give_rows(1, 3).start()

    accumulate([jnp.where(straight, p, q) for p, q in zip(group_slices(3), group_slices(1))], jnp.where(straight, 0, 1))

    @pl.when(straight)
    def _():
        trade(0).start()
        wait_near_rows(7)

    @pl.when(jnp.logical_not(straight))
    def _():
        wait_near_columns(3)

    first_half = jnp.where(straight, 1, 0)

    def nearly(f, _):
        accumulate(ends[:3], f)
        trade(f).start()
        return 0

    lax.fori_loop(first_half, 2, nearly, 0)

    @pl.when(straight)
    def _():
        wait_far_rows(7)
        give_rows(1, 4).start()
        give_columns(2).wait_recv()
        give_rows(1, 4).wait_recv()

    @pl.when(jnp.logical_not(straight))
    def _():
        wait_far_columns(3)
        give_columns(4).start()
        give_rows(0, 2).wait_recv()
        give_rows(1, 3).wait_recv()
        give_columns(4).wait_recv()

    def last(f, _):
        place = half_place(f)
        span = pl.ds(pl.multiple_of(core * width, width), width)
        left = jnp.concatenate([row[final, e, place, :] for e in range(SECTIONS)]
                               + [other_row[e, place, :] for e in range(SECTIONS)], axis=1)
        right = jnp.concatenate([col[final, e, span, :] for e in range(SECTIONS)]
                                + [other_col[e, span, :] for e in range(SECTIONS)], axis=1)
        acc[core, place, :] += lax.dot_general(
            left, right, (((1,), (1,)), ((), ())), preferred_element_type=jnp.float32)
        return 0

    lax.fori_loop(first_half, 2, last, 0)

    def settle(f, _):
        trade(f).wait_recv()
        first = lax.rem(b + f, 2) * (tiles // 2)

        def finish(t, _):
            tile_row = first + t
            place = pl.ds(pl.multiple_of(tile_row * TILE, TILE), TILE)
            for c in range(width // TILE):
                span = pl.ds(c * TILE, TILE)
                keep = mask_ref[c, tile_row].astype(jnp.float32)
                out_ref[place, span] = (acc[core, place, span] + got[place, span]) * keep
            return 0

        lax.fori_loop(0, tiles // 2, finish, 0)
        trade(f).wait_send()
        return 0

    lax.fori_loop(0, 2, settle, 0)

    @pl.when(straight)
    def _():
        give_columns(2).wait_send()
        give_rows(1, 4).wait_send()

    @pl.when(jnp.logical_not(straight))
    def _():
        give_rows(0, 2).wait_send()
        give_rows(1, 3).wait_send()
        give_columns(4).wait_send()

    part = row_part(0, 0, 0)
    whole = row_half(0, 0)
    for n in range(3):
        send(whole, whole, zs.at[0, n], zr.at[0, 0], dev_x_up).wait_send()
        for way in range(2):
            due, one = pass_along_z(n + 1, way)

            @pl.when(due)
            def _():
                one.wait_send()

    def drain_x(i, _):
        for way in range(2):
            for n in range(3):
                send(part, part, xs.at[way, i, n], xr.at[0, 0, 0], dev_x_up).wait_send()
        return 0

    lax.fori_loop(0, 8, drain_x, 0)

    @pl.when(straight)
    def _():
        def drain(n, _):
            for q in range(2):
                hops = ring if q == 0 else lax.rem(4 - ring, 4)

                @pl.when(hops < 3)
                def _():
                    send(part, part, ys.at[q, n, 0], xr.at[0, 0, 0], dev_x_up).wait_send()
            return 0

        lax.fori_loop(0, 16, drain, 0)

    @pl.when(jnp.logical_not(straight))
    def _():
        def drain(j, _):
            for way in range(2):
                for n in range(4):
                    done = (n < 2) | ((n == 2) & ((ring != 0) | (j >= RELIEVED)))

                    @pl.when(done | ((n == 3) & (ring == 2) & (j < RELIEVED)))
                    def _():
                        send(part, part, ys.at[way, j, n], xr.at[0, 0, 0], dev_x_up).wait_send()
            for n in range(8):
                @pl.when((ring == 0) | (n >= 6) | ((n == 0) & (ring != 2)))
                def _():
                    send(part, part, cs.at[j, n], xr.at[0, 0, 0], dev_x_up).wait_send()
            return 0

        lax.fori_loop(0, 4, drain, 0)


def shards(a_values, a_pattern, c_mask):
    rows, depth = a_values.shape[1], a_values.shape[2]
    out_width = c_mask.shape[1] * TILE
    half = rows // 2
    vmem = pl.BlockSpec(memory_space=pltpu.VMEM)
    dma = pltpu.SemaphoreType.DMA
    return pl.pallas_call(
        functools.partial(kernel, rows),
        out_shape=jax.ShapeDtypeStruct((rows, out_width), jnp.float32),
        in_specs=[pl.BlockSpec(memory_space=pl.ANY)] * 3,
        out_specs=vmem,
        scratch_shapes=[
            pltpu.SMEM((SECTIONS, 1, rows // TILE), jnp.int32),
            pltpu.SMEM((c_mask.shape[1], rows // TILE), jnp.int32),
            pltpu.VMEM((16, SECTIONS, rows, depth), jnp.bfloat16),
            pltpu.VMEM((16, SECTIONS, half, depth), jnp.bfloat16),
            pltpu.VMEM((2, rows, out_width), jnp.float32),
            pltpu.VMEM((rows, out_width), jnp.float32),
            pltpu.VMEM((4, 2, SECTIONS, half // 2, depth), jnp.bfloat16),
            pltpu.VMEM((4, SECTIONS, half // 2, depth), jnp.bfloat16),
            pltpu.VMEM((SECTIONS, rows, depth), jnp.bfloat16),
            pltpu.VMEM((SECTIONS, half, depth), jnp.bfloat16),
            dma((3, 3)), dma((4, 2)), dma((2, 8, 3)), dma((16, 2, 2)),
            dma((2, 16, 4)), dma((16, 2)), dma((4, 8)), dma((4, 2)), dma((4,)), dma((5,)), dma((5,)), dma((4,)),
        ],
        compiler_params=pltpu.CompilerParams(
            collective_id=0, has_side_effects=True, vmem_limit_bytes=48 << 20),
        cost_estimate=pl.CostEstimate(
            flops=2 * rows * half * 16 * SECTIONS * depth, bytes_accessed=4 * rows * out_width, transcendentals=0),
        name="gather_and_multiply",
    )(a_values, a_pattern.transpose(0, 2, 1), c_mask.T)


def solution(mesh):
    return jax.shard_map(
        shards,
        mesh=mesh,
        in_specs=(P(None, "row", "col"), P(None, "row", "col"), P("row", "col")),
        out_specs=P("row", "col"),
        check_vma=False,
    )
```
